256 devices in a mesh: dp: 8 (over y, x_lo), expert: 32 (over z, x_hi, core).
Axes of the slice: x: 4 (x_hi: 2, x_lo: 2; x = x_hi * 2 + x_lo), y: 4, z: 8, core: 2. Of those that a mesh axis runs over, the one named last changes fastest.
Arguments:
- tokens: bfloat16 [32768, 2048], P(('dp', 'expert')), may hold values from -6 to 6
- output_gradient: bfloat16 [32768, 2048], P(('dp', 'expert')), may hold values from -6 to 6
- chosen_expert_index: int32 [32768, 6], P(('dp', 'expert')), may hold values from 0 to 31, all different within a row; in each aligned block of 128 rows (0 to 127, 128 to 255, ...) at most 30 rows name the same one
- router_weight: float32 [32768, 6], P(('dp', 'expert')), may hold values from 0.05 to 0.6
- gate_weight: bfloat16 [32, 2048, 704], P('expert'), may hold values from -0.125 to 0.125
- up_weight: bfloat16 [32, 2048, 704], P('expert'), may hold values from -0.125 to 0.125
- down_weight: bfloat16 [32, 704, 2048], P('expert'), may hold values from -0.21875 to 0.21875
- adapter_down_first: float32 [32, 704, 32], P('expert', 'dp'), may hold values from -0.21875 to 0.21875
- adapter_down_second: float32 [32, 32, 2048], P('expert', None, 'dp'), may hold values from -1 to 1
- first_mean_a: float32 [32, 704, 32], P('expert', 'dp'), may hold values from -24 to 24
- squared_mean_a: float32 [32, 704, 32], P('expert', 'dp'), may hold values from 4 to 64
- first_mean_b: float32 [32, 32, 2048], P('expert', None, 'dp'), may hold values from -24 to 24
- squared_mean_b: float32 [32, 32, 2048], P('expert', None, 'dp'), may hold values from 4 to 64
Outputs:
- token_grad: bfloat16 [32768, 2048], P(('dp', 'expert'))
- updated_mean_a: float32 [32, 704, 32], P('expert', 'dp')
- updated_squared_a: float32 [32, 704, 32], P('expert', 'dp')
- adam_delta_first: float32 [32, 704, 32], P('expert', 'dp')
- updated_mean_b: float32 [32, 32, 2048], P('expert', None, 'dp')
- updated_squared_b: float32 [32, 32, 2048], P('expert', None, 'dp')
- adam_delta_second: float32 [32, 32, 2048], P('expert', None, 'dp')
The draws below stay inside these ranges and needn't reach their ends.
Inputs may be any that keep to these rules, and one draw needn't show every extreme that they name: `chosen_expert_index`: each token names 6 different experts. Among the 128 tokens of one device (aligned blocks of 128 rows) no expert is named more than 30 times, and in every draw some device names some expert exactly 30 times.
All inputs are finite; a program needn't handle non-finite values.
Results may differ from the reference program's by a relative error of at most 0.02.
Values may be sent and summed in bfloat16 or wider, within the bound.
A program may use at most 128 MiB of HBM per device.

```python
import math
import jax
import jax.numpy as jnp
import numpy as np
from jax import lax

HIDDEN_WIDTH = 2048
EXPERT_UNITS = 704
ADAPTER_RANK = 32
TOP = 6
TOK_DEV = 128
EXPERT_TOTAL = 32
TOKENS = 32768
CAP = 30


def level_of(stream_key, extent, pieces, least, high):
    loudness = 1.0
    for position, shards_of in pieces:
        steps = jax.random.uniform(jax.random.fold_in(jax.random.fold_in(stream_key, 6), position), (shards_of,), jnp.float32, least / len(pieces), high / len(pieces))
        loudness = loudness * jnp.repeat(jnp.exp(steps), extent[position] // shards_of).reshape((-1,) + (1,) * (len(extent) - 1 - position))
    return loudness


def assign_block(stream_key, own, number, rows, amount, top, bound, skew):
    order = jax.random.permutation(stream_key, amount)
    heavy_load, usual = shares(amount, rows * top, bound, skew, True), shares(amount, rows * top, bound, skew, False)
    places = jnp.arange(amount)

    def named(sizes, offset_by):
        used = int((sizes > 0).sum())
        fixed = max(1, used // 4)
        moved = fixed + (places - fixed + offset_by * (used - fixed)) % max(1, amount - fixed)
        return jnp.zeros((amount,), jnp.int32).at[order[jnp.where(places < fixed, places, moved)]].set(jnp.asarray(sizes, jnp.int32))

    sizes = jnp.where(number % 4 == 0, named(heavy_load, number // 4), named(usual, number - number // 4 - 1))
    mixed = jax.random.permutation(jax.random.fold_in(own, 3), amount)
    source_of, taker = mixed[0:amount // 2 * 2:2], mixed[1:amount // 2 * 2:2]
    slack = jnp.minimum(sizes[source_of] - 1, bound - sizes[taker]) // 2
    slack = jnp.where((source_of == order[0]) | (taker == order[0]) | (sizes[taker] == 0), 0, jnp.maximum(slack, 0))
    moved = jax.random.randint(jax.random.fold_in(own, 4), (amount // 2,), 0, 1 << 20) % (slack + 1)
    sizes = sizes.at[source_of].add(-moved).at[taker].add(moved)
    labels = jnp.searchsorted(jnp.cumsum(sizes), jnp.arange(rows * top), side="right").astype(jnp.int32)
    listing = labels.reshape(top, rows).T
    listing = listing[jax.random.permutation(jax.random.fold_in(own, 1), rows)]
    offset_by = jax.random.randint(jax.random.fold_in(own, 2), (rows, 1), 0, top)
    return jnp.take_along_axis(listing, (jnp.arange(top)[None, :] + offset_by) % top, axis=1)


def shares(number_of, total, reach, slope, full):
    portions = [(1 << 20) // math.isqrt(standing ** slope) + 1 for standing in range(1, number_of + 1)]
    largest = reach if full else min(reach, max(-(-total // number_of), total * portions[0] // sum(portions)))
    least = 1 if total - largest >= number_of - 1 else 0
    given, spare = [largest] + [least] * (number_of - 1), total - largest - least * (number_of - 1)
    while spare > 0:
        movable = [i for i in range(1, number_of) if given[i] < largest] or [i for i in range(1, number_of) if given[i] < reach]
        whole, left = sum([portions[i] for i in movable]), spare
        for i in movable:
            extra = min(reach - given[i], max(1, left * portions[i] // whole), spare)
            given[i] = given[i] + extra
            spare = spare - extra
    return np.array(given)


def bell_draw(stream_key, extent, deviation, most, cuts=(), held_as=jnp.bfloat16):
    values = jax.random.normal(stream_key, extent, jnp.float32) * deviation
    if len(cuts) > 0:
        values = level_of(stream_key, extent, cuts, -0.22, 0.18) * values
    return jnp.clip(values, min=-most, max=most).astype(held_as)


def setup_inputs(seed: int = 0) -> dict:
    streams_of = jax.random.split(jax.random.key(seed), 14)
    tokens = bell_draw(streams_of[0], (TOKENS, HIDDEN_WIDTH), 1.0, 6.0, ((0, 256),))
    output_gradient = bell_draw(streams_of[1], (TOKENS, HIDDEN_WIDTH), 1.0, 6.0, ((0, 256),))
    chosen_expert_index_keys = jax.random.split(jax.random.fold_in(streams_of[2], 1), TOKENS // TOK_DEV)
    chosen_expert_index_turns = jax.random.permutation(jax.random.fold_in(streams_of[2], 3), TOKENS // TOK_DEV)
    chosen_expert_index = jax.vmap(lambda own, number: assign_block(jax.random.fold_in(streams_of[2], 2), own, number, TOK_DEV, EXPERT_TOTAL, TOP, CAP, 2))(chosen_expert_index_keys, chosen_expert_index_turns).reshape((TOKENS, TOP))
    router_weight = jnp.clip(0.05 + 0.55 * jax.random.uniform(streams_of[3], (TOKENS, TOP), jnp.float32) ** level_of(streams_of[3], (TOKENS, TOP), ((0, 256),), -0.2, 0.2), 0.05, 0.6)
    gate_weight = bell_draw(streams_of[4], (EXPERT_TOTAL, HIDDEN_WIDTH, EXPERT_UNITS), HIDDEN_WIDTH ** -0.5, 0.125, ((0, 32),))
    up_weight = bell_draw(streams_of[5], (EXPERT_TOTAL, HIDDEN_WIDTH, EXPERT_UNITS), HIDDEN_WIDTH ** -0.5, 0.125, ((0, 32),))
    down_weight = bell_draw(streams_of[6], (EXPERT_TOTAL, EXPERT_UNITS, HIDDEN_WIDTH), EXPERT_UNITS ** -0.5, 0.21875, ((0, 32),))
    adapter_down_first = bell_draw(streams_of[7], (EXPERT_TOTAL, EXPERT_UNITS, ADAPTER_RANK), EXPERT_UNITS ** -0.5, 0.21875, ((0, 32), (1, 8)), jnp.float32)
    adapter_down_second = bell_draw(streams_of[8], (EXPERT_TOTAL, ADAPTER_RANK, HIDDEN_WIDTH), ADAPTER_RANK ** -0.5, 1.0, ((0, 32), (2, 8)), jnp.float32)
    first_mean_a = bell_draw(streams_of[9], (EXPERT_TOTAL, EXPERT_UNITS, ADAPTER_RANK), 4.0, 24.0, ((0, 32), (1, 8)), jnp.float32)
    squared_mean_a = jnp.clip(jnp.exp(math.log(64.0) - 2.7725887 * jax.random.uniform(streams_of[10], (EXPERT_TOTAL, EXPERT_UNITS, ADAPTER_RANK), jnp.float32) ** level_of(streams_of[10], (EXPERT_TOTAL, EXPERT_UNITS, ADAPTER_RANK), ((0, 32), (1, 8)), -0.2, 0.2)), 4.0, 64.0)
    first_mean_b = bell_draw(streams_of[11], (EXPERT_TOTAL, ADAPTER_RANK, HIDDEN_WIDTH), 4.0, 24.0, ((0, 32), (2, 8)), jnp.float32)
    squared_mean_b = jnp.clip(jnp.exp(math.log(64.0) - 2.7725887 * jax.random.uniform(streams_of[12], (EXPERT_TOTAL, ADAPTER_RANK, HIDDEN_WIDTH), jnp.float32) ** level_of(streams_of[12], (EXPERT_TOTAL, ADAPTER_RANK, HIDDEN_WIDTH), ((0, 32), (2, 8)), -0.2, 0.2)), 4.0, 64.0)
    return {"tokens": tokens, "output_gradient": output_gradient, "chosen_expert_index": chosen_expert_index, "router_weight": router_weight, "gate_weight": gate_weight, "up_weight": up_weight, "down_weight": down_weight, "adapter_down_first": adapter_down_first, "adapter_down_second": adapter_down_second, "first_mean_a": first_mean_a, "squared_mean_a": squared_mean_a, "first_mean_b": first_mean_b, "squared_mean_b": squared_mean_b}


adapter_scale = 2.0
beta_one = 0.9
beta_two = 0.999
bias_one = 1.0 - math.exp(1000.0 * math.log(0.9))
bias_two = 1.0 - math.exp(1000.0 * math.log(0.999))
adam_eps = 1e-08
weight_decay = 0.1
ref_rows = 1024

def expert_pass(rows_in, row_gradients, gate_mat, up_mat, down_mat, first_adapter, second_adapter):
    contract_trailing = (((1,), (1,)), ((), ()))
    contract_leading = (((0,), (0,)), ((), ()))
    gate_pre = jnp.dot(rows_in, gate_mat, preferred_element_type=jnp.float32)
    up_pre = jnp.dot(rows_in, up_mat, preferred_element_type=jnp.float32)
    sigmoid_gate = jax.nn.sigmoid(gate_pre)
    activated = gate_pre * sigmoid_gate
    expert_activation = (activated * up_pre).astype(jnp.bfloat16)
    narrow_product = jnp.dot(expert_activation, first_adapter, preferred_element_type=jnp.float32).astype(jnp.bfloat16)
    narrow_gradient = lax.dot_general(row_gradients, second_adapter, contract_trailing, preferred_element_type=jnp.float32).astype(jnp.bfloat16)
    activation_gradient = lax.dot_general(row_gradients, down_mat, contract_trailing, preferred_element_type=jnp.float32)
    activation_gradient = activation_gradient + adapter_scale * lax.dot_general(narrow_gradient, first_adapter, contract_trailing, preferred_element_type=jnp.float32)
    gate_grad = (activation_gradient * up_pre * sigmoid_gate * (1.0 + gate_pre * (1.0 - sigmoid_gate))).astype(jnp.bfloat16)
    up_grad = (activation_gradient * activated).astype(jnp.bfloat16)
    input_grad = lax.dot_general(gate_grad, gate_mat, contract_trailing, preferred_element_type=jnp.float32)
    input_grad = (input_grad + lax.dot_general(up_grad, up_mat, contract_trailing, preferred_element_type=jnp.float32)).astype(jnp.bfloat16)
    first_factor_gradient = adapter_scale * lax.dot_general(expert_activation, narrow_gradient, contract_leading, preferred_element_type=jnp.float32)
    second_factor_gradient = adapter_scale * lax.dot_general(narrow_product, row_gradients, contract_leading, preferred_element_type=jnp.float32)
    return (input_grad, first_factor_gradient, second_factor_gradient)

def decoupled_adam_update(param, grad, moment, second):
    moment_new = beta_one * moment + (1.0 - beta_one) * grad
    second_new = beta_two * second + (1.0 - beta_two) * grad * grad
    update = moment_new / bias_one / (jnp.sqrt(second_new / bias_two) + adam_eps) + weight_decay * param
    return (moment_new, second_new, update)

def reference(tokens, output_gradient, chosen_expert_index, router_weight, gate_weight, up_weight, down_weight, adapter_down_first, adapter_down_second, first_mean_a, squared_mean_a, first_mean_b, squared_mean_b):
    pair_total = TOKENS * TOP
    chosen = chosen_expert_index.reshape(-1).astype(jnp.int32)
    sorted_pairs = jnp.argsort(chosen, stable=True).astype(jnp.int32)
    expert_load = jnp.zeros((EXPERT_TOTAL,), jnp.int32).at[chosen].add(1)
    first_row = (jnp.cumsum(expert_load) - expert_load).astype(jnp.int32)
    pair_weight = router_weight.reshape(-1)
    first_adapter = adapter_down_first.astype(jnp.bfloat16)
    second_adapter = adapter_down_second.astype(jnp.bfloat16)

    def per_expert(grad_sum, expert):
        gate_mat = lax.dynamic_index_in_dim(gate_weight, expert, 0, keepdims=False)
        up_mat = lax.dynamic_index_in_dim(up_weight, expert, 0, keepdims=False)
        down_mat = lax.dynamic_index_in_dim(down_weight, expert, 0, keepdims=False)
        factor_a = lax.dynamic_index_in_dim(first_adapter, expert, 0, keepdims=False)
        factor_b = lax.dynamic_index_in_dim(second_adapter, expert, 0, keepdims=False)
        row_count = expert_load[expert]
        row_first = first_row[expert]
        block_total = (row_count + ref_rows - 1) // ref_rows

        def one_block(block_index, running):
            grad_acc, total_a, total_b = running
            offsets = (block_index * ref_rows + jnp.arange(ref_rows, dtype=jnp.int32)).astype(jnp.int32)
            valid_row = offsets < row_count
            pair_index = sorted_pairs[jnp.clip(row_first + offsets, 0, pair_total - 1).astype(jnp.int32)]
            token_index = (pair_index // TOP).astype(jnp.int32)
            rows_in = jnp.where(valid_row[:, None], tokens[token_index], jnp.zeros((), tokens.dtype))
            scaled = pair_weight[pair_index][:, None] * output_gradient[token_index].astype(jnp.float32)
            row_gradients = jnp.where(valid_row[:, None], scaled, jnp.zeros((), jnp.float32)).astype(jnp.bfloat16)
            input_grad, part_a, part_b = expert_pass(rows_in, row_gradients, gate_mat, up_mat, down_mat, factor_a, factor_b)
            masked = jnp.where(valid_row[:, None], input_grad.astype(jnp.float32), jnp.zeros((), jnp.float32))
            grad_acc = grad_acc.at[token_index].add(masked)
            return (grad_acc, total_a + part_a, total_b + part_b)
        start_state = (grad_sum, jnp.zeros((EXPERT_UNITS, ADAPTER_RANK), jnp.float32), jnp.zeros((ADAPTER_RANK, HIDDEN_WIDTH), jnp.float32))
        grad_sum, total_a, total_b = lax.fori_loop(0, block_total, one_block, start_state)
        return (grad_sum, (total_a, total_b))
    grad_sum, (first_factor_gradient, second_factor_gradient) = lax.scan(per_expert, jnp.zeros((TOKENS, HIDDEN_WIDTH), jnp.float32), jnp.arange(EXPERT_TOTAL, dtype=jnp.int32))
    token_grad = grad_sum.astype(jnp.bfloat16)
    updated_mean_a, updated_squared_a, adam_delta_first = decoupled_adam_update(adapter_down_first, first_factor_gradient, first_mean_a, squared_mean_a)
    updated_mean_b, updated_squared_b, adam_delta_second = decoupled_adam_update(adapter_down_second, second_factor_gradient, first_mean_b, squared_mean_b)
    return (token_grad, updated_mean_a, updated_squared_a, adam_delta_first, updated_mean_b, updated_squared_b, adam_delta_second)
```

```python
import math

import jax
import jax.numpy as jnp
from jax import lax
from jax.sharding import PartitionSpec as P

adapter_scale = 2.0
beta_one = 0.9
beta_two = 0.999
bias_one = 1.0 - math.exp(1000.0 * math.log(0.9))
bias_two = 1.0 - math.exp(1000.0 * math.log(0.999))
adam_eps = 1e-08
weight_decay = 0.1


def expert_pass(rows_in, row_gradients, gate_mat, up_mat, down_mat, first_adapter, second_adapter):
    contract_trailing = (((1,), (1,)), ((), ()))
    contract_leading = (((0,), (0,)), ((), ()))
    gate_pre = jnp.dot(rows_in, gate_mat, preferred_element_type=jnp.float32)
    up_pre = jnp.dot(rows_in, up_mat, preferred_element_type=jnp.float32)
    sigmoid_gate = jax.nn.sigmoid(gate_pre)
    activated = gate_pre * sigmoid_gate
    expert_activation = (activated * up_pre).astype(jnp.bfloat16)
    narrow_product = jnp.dot(
        expert_activation, first_adapter, preferred_element_type=jnp.float32
    ).astype(jnp.bfloat16)
    narrow_gradient = lax.dot_general(
        row_gradients, second_adapter, contract_trailing, preferred_element_type=jnp.float32
    ).astype(jnp.bfloat16)
    activation_gradient = lax.dot_general(
        row_gradients, down_mat, contract_trailing, preferred_element_type=jnp.float32
    )
    activation_gradient = activation_gradient + adapter_scale * lax.dot_general(
        narrow_gradient, first_adapter, contract_trailing, preferred_element_type=jnp.float32
    )
    gate_grad = (
        activation_gradient * up_pre * sigmoid_gate * (1.0 + gate_pre * (1.0 - sigmoid_gate))
    ).astype(jnp.bfloat16)
    up_grad = (activation_gradient * activated).astype(jnp.bfloat16)
    input_grad = lax.dot_general(
        gate_grad, gate_mat, contract_trailing, preferred_element_type=jnp.float32
    )
    input_grad = (
        input_grad
        + lax.dot_general(up_grad, up_mat, contract_trailing, preferred_element_type=jnp.float32)
    ).astype(jnp.bfloat16)
    first_factor_gradient = adapter_scale * lax.dot_general(
        expert_activation, narrow_gradient, contract_leading, preferred_element_type=jnp.float32
    )
    second_factor_gradient = adapter_scale * lax.dot_general(
        narrow_product, row_gradients, contract_leading, preferred_element_type=jnp.float32
    )
    return (input_grad, first_factor_gradient, second_factor_gradient)


def decoupled_adam_update(param, grad, moment, second):
    moment_new = beta_one * moment + (1.0 - beta_one) * grad
    second_new = beta_two * second + (1.0 - beta_two) * grad * grad
    update = (
        moment_new / bias_one / (jnp.sqrt(second_new / bias_two) + adam_eps) + weight_decay * param
    )
    return (moment_new, second_new, update)


def shards(
    tokens,
    output_gradient,
    chosen_expert_index,
    router_weight,
    gate_weight,
    up_weight,
    down_weight,
    adapter_down_first,
    adapter_down_second,
    first_mean_a,
    squared_mean_a,
    first_mean_b,
    squared_mean_b,
):
    token_count, model_width = tokens.shape
    top_count = chosen_expert_index.shape[1]
    expert_count = lax.axis_size("expert")
    capacity = min(token_count, 5 * token_count * top_count // (4 * expert_count))
    slot_total = expert_count * capacity
    chosen = chosen_expert_index.reshape(-1)
    one_hot = (chosen[:, None] == jnp.arange(expert_count, dtype=jnp.int32)[None, :]).astype(
        jnp.int32
    )
    pair_number = jnp.arange(token_count * top_count, dtype=jnp.int32)
    earlier = (pair_number[None, :] < pair_number[:, None]).astype(jnp.bfloat16)
    before = jnp.dot(
        earlier, one_hot.astype(jnp.bfloat16), preferred_element_type=jnp.float32
    ).astype(jnp.int32)
    rank_in = jnp.sum(before * one_hot, axis=1)
    slot_of = chosen * capacity + rank_in
    per_expert = jnp.sum(one_hot, axis=0).reshape(expert_count, 1)
    source_rows = jnp.arange(token_count * top_count, dtype=jnp.int32) // top_count
    picked = tokens[source_rows]
    scaled = (
        router_weight.reshape(-1)[:, None] * output_gradient[source_rows].astype(jnp.float32)
    ).astype(jnp.bfloat16)
    send_rows = jnp.zeros((slot_total, model_width), jnp.bfloat16).at[slot_of].set(picked)
    send_grads = jnp.zeros((slot_total, model_width), jnp.bfloat16).at[slot_of].set(scaled)
    recv_rows, recv_grads, recv_counts = (
        lax.all_to_all(send_rows, "expert", split_axis=0, concat_axis=0, tiled=True),
        lax.all_to_all(send_grads, "expert", split_axis=0, concat_axis=0, tiled=True),
        lax.all_to_all(per_expert, "expert", split_axis=0, concat_axis=0, tiled=True),
    )
    full_a, full_b = (
        lax.all_gather(adapter_down_first.astype(jnp.bfloat16), "dp", axis=1, tiled=True),
        lax.all_gather(adapter_down_second.astype(jnp.bfloat16), "dp", axis=2, tiled=True),
    )
    gate_mat = gate_weight[0]
    up_mat = up_weight[0]
    down_mat = down_weight[0]
    factor_a = full_a[0]
    factor_b = full_b[0]
    slot_grads, first_factor_gradient, second_factor_gradient = expert_pass(
        recv_rows, recv_grads, gate_mat, up_mat, down_mat, factor_a, factor_b
    )
    returned = lax.all_to_all(slot_grads, "expert", split_axis=0, concat_axis=0, tiled=True)
    gathered = returned[slot_of].astype(jnp.float32).reshape(token_count, top_count, model_width)
    token_grad = jnp.sum(gathered, axis=1).astype(jnp.bfloat16)
    local_first_factor, local_second_factor = (
        lax.psum_scatter(
            first_factor_gradient.astype(jnp.bfloat16), "dp", scatter_dimension=0, tiled=True
        ).astype(jnp.float32),
        lax.psum_scatter(
            second_factor_gradient.astype(jnp.bfloat16), "dp", scatter_dimension=1, tiled=True
        ).astype(jnp.float32),
    )
    updated_mean_a, updated_squared_a, adam_delta_first = decoupled_adam_update(
        adapter_down_first[0], local_first_factor, first_mean_a[0], squared_mean_a[0]
    )
    updated_mean_b, updated_squared_b, adam_delta_second = decoupled_adam_update(
        adapter_down_second[0], local_second_factor, first_mean_b[0], squared_mean_b[0]
    )
    return (
        token_grad,
        updated_mean_a[None],
        updated_squared_a[None],
        adam_delta_first[None],
        updated_mean_b[None],
        updated_squared_b[None],
        adam_delta_second[None],
    )


def solution(mesh):
    placed = (
        P(("dp", "expert"), None),
        P(("dp", "expert"), None),
        P(("dp", "expert"), None),
        P(("dp", "expert"), None),
        P("expert", None, None),
        P("expert", None, None),
        P("expert", None, None),
        P("expert", "dp", None),
        P("expert", None, "dp"),
        P("expert", "dp", None),
        P("expert", "dp", None),
        P("expert", None, "dp"),
        P("expert", None, "dp"),
    )
    return jax.shard_map(
        shards,
        mesh=mesh,
        in_specs=placed,
        out_specs=(
            P(("dp", "expert"), None),
            P("expert", "dp", None),
            P("expert", "dp", None),
            P("expert", "dp", None),
            P("expert", None, "dp"),
            P("expert", None, "dp"),
            P("expert", None, "dp"),
        ),
        check_vma=False,
    )
```

```python
import functools
import math

import jax
import jax.numpy as jnp
from jax import lax
from jax.experimental import pallas as pl
from jax.experimental.pallas import tpu as pltpu
from jax.sharding import PartitionSpec as P

adapter_scale = 2.0
beta_one = 0.9
beta_two = 0.999
bias_one = 1.0 - math.exp(1000.0 * math.log(0.9))
bias_two = 1.0 - math.exp(1000.0 * math.log(0.999))
adam_eps = 1e-08
weight_decay = 0.1

MESH = pl.DeviceIdType.MESH
NT = (((1,), (1,)), ((), ()))
NN = (((1,), (0,)), ((), ()))
TN = (((0,), (0,)), ((), ()))
RING = 8
SLOT = 32
RANK = 32
PART = 384
f32 = jnp.float32
bf16 = jnp.bfloat16


def dot(a, b, dims=NN):
    return lax.dot_general(a, b, dims, preferred_element_type=f32)


def kernel(
    tok_ref, grad_ref, chosen_ref, weight_ref, gate_ref, up_ref, down_ref, shard_ref,
    out_ref, sum_ref,
    tg, wg, wu, wd, ab, gs, gr, ms, mr, rp, rm, factor,
    ag_send, ag_recv, w_send, w_recv, rs_send, rs_recv, ab_send, ab_recv,
    gab_send, gab_recv, m_send, m_recv, own_sem,
):
    tokens, width = tok_ref.shape
    units = gate_ref.shape[2]
    half = width // 2
    dp = lax.axis_index("dp")
    ex = lax.axis_index("expert")
    z, xh, core = ex // 4, (ex // 2) % 2, ex % 2
    y, xl = dp // 2, dp % 2

    def at(zz, hh, cc):
        return (zz * 2 + hh) * 2 + cc

    zp = (dp, at((z + 1) % RING, xh, core))
    zm = (dp, at((z + RING - 1) % RING, xh, core))
    sib = (dp, at(z, xh, 1 - core))
    cross = (y * 2 + 1 - xl, at(z, 1 - xh, core))
    xlo = (y * 2 + 1 - xl, ex)
    yp = (((y + 1) % 4) * 2 + xl, ex)
    ym = (((y + 3) % 4) * 2 + xl, ex)

    def plane(k, j):
        hh = xh if k < 2 else 1 - xh
        cc = core if k % 2 == 0 else 1 - core
        return ((dp + j) % 8, at(z, hh, cc))

    def each_peer(f):
        for k in range(4):
            lax.fori_loop(1 if k == 0 else 0, 8, functools.partial(lambda k, j, c: (f(k, j), c)[1], k), 0)

    barrier = pltpu.get_barrier_semaphore()

    def greet(device):
        pl.semaphore_signal(barrier, inc=1, device_id=device, device_id_type=MESH)

    each_peer(lambda k, j: greet(plane(k, j)))
    lax.fori_loop(1, RING, lambda r, c: (greet((dp, at((z + r) % RING, xh, core))), c)[1], 0)
    pl.semaphore_wait(barrier, 31 + RING - 1)

    def remote(src, dst, send, recv, device):
        return pltpu.make_async_remote_copy(
            src_ref=src, dst_ref=dst, send_sem=send, recv_sem=recv, device_id=device, device_id_type=MESH
        )

    def piece(ref, h):
        return ref.at[:, pl.ds(h * half, half)]

    def ag(a, way, hop, h):
        own = tok_ref if a == 0 else grad_ref
        here = hop if way == 0 else (RING - hop) % RING
        there = hop + 1 if way == 0 else RING - hop - 1
        src = own if hop == 0 else tg.at[a, here]
        return remote(
            piece(src, h), piece(tg.at[a, there], h), ag_send.at[a, way, hop, h],
            ag_recv.at[a, there, h], zp if way == 0 else zm,
        )

    def ag_has(hop, way, h):
        return hop < 3 or h == way

    for a in range(2):
        for h in range(2):
            for way in range(2):
                ag(a, way, 0, h).start()
    own_tok = pltpu.make_async_copy(tok_ref, tg.at[0, 0], own_sem.at[0])
    own_grad = pltpu.make_async_copy(grad_ref, tg.at[1, 0], own_sem.at[1])
    own_tok.start()
    own_grad.start()

    own_w = (gate_ref.at[0], up_ref.at[0], down_ref.at[0])
    all_w = (wg, wu, wd)

    def part(ref, m, q, n):
        size = width // 8 * n
        begin = pl.ds(pl.multiple_of(q * (width // 8), width // 8), size)
        return ref.at[begin, :] if m < 2 else ref.at[:, begin]

    c_piece = y * 2 + 1 - xl
    s_piece = y * 2 + xl

    def piece_of(row, name):
        return (row % 4) * 2 + (1 - xl if name == 0 else xl)

    def w_copy(m, n):
        src2 = all_w[m].at[2]
        if n == 0:
            return remote(own_w[m], all_w[m].at[1], w_send.at[m, 0], w_recv.at[m, 0], sib)
        if n == 1:
            return remote(part(own_w[m], m, dp, 1), part(src2, m, dp, 1), w_send.at[m, 1], w_recv.at[m, 1], cross)
        if n == 2:
            return remote(part(src2, m, c_piece, 1), part(src2, m, c_piece, 1), w_send.at[m, 2], w_recv.at[m, 2], xlo)
        if n < 9:
            q = {
                3: piece_of(y, 0), 4: piece_of(y, 1), 5: piece_of(y, 0), 6: piece_of(y, 1),
                7: piece_of(y + 3, 0), 8: piece_of(y + 1, 1),
            }[n]
            device = yp if n in (3, 4, 7) else ym
            return remote(part(src2, m, q, 1), part(src2, m, q, 1), w_send.at[m, n], w_recv.at[m, n], device)
        row = (y + (0, 3, 1, 2)[n - 9]) % 4
        return remote(
            part(src2, m, row * 2, 2), part(all_w[m].at[3], m, row * 2, 2), w_send.at[m, n], w_recv.at[m, n], sib
        )

    own_copies = [pltpu.make_async_copy(own_w[m], all_w[m].at[0], own_sem.at[2 + m]) for m in range(3)]
    for m in range(3):
        w_copy(m, 1).start()
    for m in range(3):
        w_copy(m, 0).start()
        own_copies[m].start()

    ab[pl.ds(dp, 1)] = shard_ref[...][None]

    def ab_copy(k, j):
        return remote(shard_ref, ab.at[k * 8 + dp], ab_send, ab_recv, plane(k, j))

    each_peer(lambda k, j: ab_copy(k, j).start())

    ids = lax.broadcasted_iota(jnp.int32, (4 * RING, tokens), 0)
    named = jnp.zeros((4 * RING, tokens), f32)
    weighted = jnp.zeros((4 * RING, tokens), f32)
    for k in range(chosen_ref.shape[0]):
        hit = ids == chosen_ref[k : k + 1, :]
        named = jnp.where(hit, 1.0, named)
        weighted = jnp.where(hit, weight_ref[k : k + 1, :], weighted)
    earlier = lax.broadcasted_iota(jnp.int32, (tokens, tokens), 0) < lax.broadcasted_iota(
        jnp.int32, (tokens, tokens), 1
    )
    rank = dot(named.astype(bf16), jnp.where(earlier, 1.0, 0.0).astype(bf16))
    rank = jnp.where(named > 0.5, rank, -1.0)
    for zz in range(RING):
        ms[zz, 0:4, :] = rank[zz * 4 : zz * 4 + 4]
        ms[zz, 4:8, :] = weighted[zz * 4 : zz * 4 + 4]
    mr[pl.ds(0, 1)] = ms[pl.ds(z, 1)]

    def m_copy(r):
        there = (z + r) % RING
        return remote(ms.at[there], mr.at[r], m_send, m_recv, (dp, at(there, xh, core)))

    lax.fori_loop(1, RING, lambda r, c: (m_copy(r).start(), c)[1], 0)

    def ag_arrive(a, hop):
        for h in range(2):
            for way in range(2):
                if not ag_has(hop - 1, way, h):
                    continue
                ag(a, way, hop - 1, h).wait_recv()
                if hop < 4 and ag_has(hop, way, h):
                    ag(a, way, hop, h).start()

    for m in range(3):
        w_copy(m, 1).wait_recv()
        for n in (2, 3, 5):
            w_copy(m, n).start()
    ag_arrive(0, 1)
    for m in range(3):
        w_copy(m, 2).wait_recv()
        for n in (4, 6, 9):
            w_copy(m, n).start()
    ag_arrive(1, 1)
    ag_arrive(0, 2)
    ag_arrive(1, 2)
    for m in range(3):
        w_copy(m, 3).wait_recv()
        w_copy(m, 7).start()
        w_copy(m, 6).wait_recv()
        w_copy(m, 8).start()
    ag_arrive(0, 3)
    for m in range(3):
        w_copy(m, 4).wait_recv()
        w_copy(m, 10).start()
        w_copy(m, 5).wait_recv()
        w_copy(m, 11).start()
    ag_arrive(1, 3)
    for m in range(3):
        w_copy(m, 7).wait_recv()
        w_copy(m, 8).wait_recv()
        w_copy(m, 12).start()
    ag_arrive(0, 4)
    ag_arrive(1, 4)
    own_tok.wait()
    own_grad.wait()
    for c in own_copies:
        c.wait()
    for m in range(3):
        for n in (0, 9, 10, 11, 12):
            w_copy(m, n).wait_recv()
    for m in range(3):
        for n in range(13):
            w_copy(m, n).wait_send()
    for a in range(2):
        for hop in range(4):
            for h in range(2):
                for way in range(2):
                    if ag_has(hop, way, h):
                        ag(a, way, hop, h).wait_send()
    many = ab.at[pl.ds(0, 31)]
    pltpu.make_async_copy(many, many, ab_recv).wait()
    pltpu.make_async_copy(many, many, ab_send).wait()
    seven = mr.at[pl.ds(1, RING - 1)]
    pltpu.make_async_copy(seven, seven, m_recv).wait()
    pltpu.make_async_copy(seven, seven, m_send).wait()

    slots = lax.broadcasted_iota(jnp.int32, (SLOT, tokens), 0).astype(f32)

    def row_of(k):
        hh = xh if k < 2 else 1 - xh
        cc = core if k % 2 == 0 else 1 - core
        return hh * 2 + cc

    def picks(b):
        return [
            jnp.where(slots == mr[b, pl.ds(row_of(k), 1), :], 1.0, 0.0) for k in range(4)
        ]

    def gather(b, carry):
        chosen = picks(b)
        scale = jnp.concatenate(
            [
                jnp.sum(chosen[k] * mr[b, pl.ds(row_of(k) + 4, 1), :], axis=1, keepdims=True)
                for k in range(4)
            ],
            axis=0,
        )
        pick = jnp.concatenate(chosen, axis=0).astype(bf16)
        tg[0, b] = dot(pick, tg[0, b]).astype(bf16)
        tg[1, b] = (dot(pick, tg[1, b]) * scale).astype(bf16)
        return carry

    lax.fori_loop(0, RING, gather, 0)

    unit_count = units // 8

    def spread(d):
        i = lax.broadcasted_iota(jnp.int32, (128, units), 0)
        j = lax.broadcasted_iota(jnp.int32, (128, units), 1)
        return jnp.where((j - d * unit_count == i) & (i < unit_count), 1.0, 0.0).astype(bf16)

    def assemble(k, carry):
        def one(d, total):
            return total + dot(ab[k * 8 + d, :, 0:128], spread(d))

        factor[k] = lax.fori_loop(0, 8, one, jnp.zeros((RANK, units), f32)).astype(bf16)
        return carry

    lax.fori_loop(0, 4, assemble, 0)

    def expert(k, carry):
        where = pl.ds(pl.multiple_of(k * SLOT, SLOT), SLOT)
        rows = RING * SLOT
        x = tg[0, :, where, :].reshape(rows, width)
        g = tg[1, :, where, :].reshape(rows, width)
        a_t = factor[k]
        b_all = jnp.concatenate([ab[k * 8 + d, :, 128:PART] for d in range(8)], axis=1)
        gate_pre = dot(x, wg[k])
        up_pre = dot(x, wu[k])
        s = jax.nn.sigmoid(gate_pre)
        activated = gate_pre * s
        hidden = (activated * up_pre).astype(bf16)
        low_rank = dot(hidden, a_t, NT).astype(bf16)
        low_grad = dot(g, b_all, NT).astype(bf16)
        hidden_grad = dot(g, wd[k], NT) + adapter_scale * dot(low_grad, a_t)
        gate_grad = (hidden_grad * up_pre * s * (1.0 + gate_pre * (1.0 - s))).astype(bf16)
        up_grad = (hidden_grad * activated).astype(bf16)
        pair = dot(gate_grad, wg[k], NT) + dot(up_grad, wu[k], NT)
        tg[0, :, where, :] = pair.astype(bf16).reshape(RING, SLOT, width)
        grad_a = (adapter_scale * dot(low_grad, hidden, TN)).astype(bf16)
        grad_b = (adapter_scale * dot(low_rank, g, TN)).astype(bf16)
        for d in range(8):
            gs[k * 8 + d, :, 0:128] = dot(grad_a, spread(d), NT).astype(bf16)
            gs[k * 8 + d, :, 128:PART] = grad_b[:, d * 256 : d * 256 + 256]
        return carry

    lax.fori_loop(0, 4, expert, 0)

    def gab_copy(k, j):
        return remote(gs.at[k * 8 + (dp + j) % 8], gr.at[k * 8 + dp], gab_send, gab_recv, plane(k, j))

    each_peer(lambda k, j: gab_copy(k, j).start())

    def combine(b, carry):
        pick = jnp.concatenate(picks(b), axis=0).astype(bf16)
        tg[0, b] = dot(pick, tg[0, b], TN).astype(bf16)
        return carry

    lax.fori_loop(0, RING, combine, 0)

    def rs(way, step, h):
        here = 4 + step if way == 0 else 4 - step
        landing = rp if way == 0 else rm
        return remote(
            piece(tg.at[0, here], h), landing.at[step, h], rs_send.at[way, step, h],
            rs_recv.at[way, step, h], zp if way == 0 else zm,
        )

    def rs_add(way, step, h):
        rs(way, step, h).wait_recv()
        landing = rp if way == 0 else rm
        here = 5 + step if way == 0 else 3 - step
        cols = slice(h * half, h * half + half)
        tg[0, here, :, cols] = (tg[0, here, :, cols].astype(f32) + landing[step, h].astype(f32)).astype(bf16)
        rs(way, step + 1, h).start()

    for way in range(2):
        rs(way, 0, way).start()
        rs(way, 1, 1 - way).start()
    for step in range(3):
        for way in range(2):
            if step > 0:
                rs_add(way, step, 1 - way)
        for way in range(2):
            rs_add(way, step, way)
    for h in range(2):
        rs(0, 3, h).wait_recv()
        rs(1, 3, h).wait_recv()
        cols = slice(h * half, h * half + half)
        out_ref[:, cols] = (
            tg[0, 0, :, cols].astype(f32) + rp[3, h].astype(f32) + rm[3, h].astype(f32)
        ).astype(bf16)

    many_g = gr.at[pl.ds(0, 31)]
    pltpu.make_async_copy(many_g, many_g, gab_recv).wait()
    pltpu.make_async_copy(many_g, many_g, gab_send).wait()
    gr[pl.ds(dp, 1)] = gs[pl.ds(dp, 1)]
    sum_ref[...] = lax.fori_loop(
        0, 32, lambda i, total: total + gr[i].astype(f32), jnp.zeros((RANK, PART), f32)
    )
    for way in range(2):
        for step in range(4):
            for h in range(2):
                if step > 0 or h == way:
                    rs(way, step, h).wait_send()


def expert_layer(tokens, grads, chosen, weights, gate, up, down, shard):
    count, width = tokens.shape
    units = gate.shape[2]
    vmem = pl.BlockSpec(memory_space=pltpu.VMEM)
    hbm = pl.BlockSpec(memory_space=pl.ANY)
    dma = pltpu.SemaphoreType.DMA
    return pl.pallas_call(
        kernel,
        out_shape=(
            jax.ShapeDtypeStruct((count, width), bf16),
            jax.ShapeDtypeStruct((RANK, PART), f32),
        ),
        in_specs=[hbm, hbm, vmem, vmem, hbm, hbm, hbm, vmem],
        out_specs=(vmem, vmem),
        scratch_shapes=[
            pltpu.VMEM((2, RING, count, width), bf16),
            pltpu.VMEM((4, width, units), bf16),
            pltpu.VMEM((4, width, units), bf16),
            pltpu.VMEM((4, units, width), bf16),
            pltpu.VMEM((32, RANK, PART), bf16),
            pltpu.VMEM((32, RANK, PART), bf16),
            pltpu.VMEM((32, RANK, PART), bf16),
            pltpu.VMEM((RING, 8, count), f32),
            pltpu.VMEM((RING, 8, count), f32),
            pltpu.VMEM((4, 2, count, width // 2), bf16),
            pltpu.VMEM((4, 2, count, width // 2), bf16),
            pltpu.VMEM((4, RANK, units), bf16),
            dma((2, 2, 4, 2)),
            dma((2, 8, 2)),
            dma((3, 13)),
            dma((3, 13)),
            dma((2, 4, 2)),
            dma((2, 4, 2)),
            dma,
            dma,
            dma,
            dma,
            dma,
            dma,
            dma((5,)),
        ],
        compiler_params=pltpu.CompilerParams(
            collective_id=0, has_side_effects=True, vmem_limit_bytes=60 * 1024 * 1024
        ),
        name="expert_layer",
    )(tokens, grads, chosen, weights, gate, up, down, shard)


def decoupled_adam_update(param, grad, moment, second):
    moment_new = beta_one * moment + (1.0 - beta_one) * grad
    second_new = beta_two * second + (1.0 - beta_two) * grad * grad
    update = (
        moment_new / bias_one / (jnp.sqrt(second_new / bias_two) + adam_eps) + weight_decay * param
    )
    return (moment_new, second_new, update)


def shards(
    tokens,
    output_gradient,
    chosen_expert_index,
    router_weight,
    gate_weight,
    up_weight,
    down_weight,
    adapter_down_first,
    adapter_down_second,
    first_mean_a,
    squared_mean_a,
    first_mean_b,
    squared_mean_b,
):
    unit_count = adapter_down_first.shape[1]
    shard = jnp.concatenate(
        [
            jnp.pad(adapter_down_first[0].T, ((0, 0), (0, 128 - unit_count))),
            adapter_down_second[0],
        ],
        axis=1,
    ).astype(bf16)
    token_grad, sums = expert_layer(
        tokens,
        output_gradient,
        chosen_expert_index.T,
        router_weight.T,
        gate_weight,
        up_weight,
        down_weight,
        shard,
    )
    updated_a = decoupled_adam_update(
        adapter_down_first[0], sums[:, :unit_count].T, first_mean_a[0], squared_mean_a[0]
    )
    updated_b = decoupled_adam_update(
        adapter_down_second[0], sums[:, 128:], first_mean_b[0], squared_mean_b[0]
    )
    return (token_grad, *(v[None] for v in updated_a), *(v[None] for v in updated_b))


def solution(mesh):
    rows = P(("dp", "expert"), None)
    frozen = P("expert", None, None)
    first = P("expert", "dp", None)
    second = P("expert", None, "dp")
    return jax.shard_map(
        shards,
        mesh=mesh,
        in_specs=(rows,) * 4 + (frozen,) * 3 + (first, second, first, first, second, second),
        out_specs=(rows, first, first, first, second, second, second),
        check_vma=False,
    )
```

```python
import functools
import math

import jax
import jax.numpy as jnp
from jax import lax
from jax.experimental import pallas as pl
from jax.experimental.pallas import tpu as pltpu
from jax.sharding import PartitionSpec as P

adapter_scale = 2.0
beta_one = 0.9
beta_two = 0.999
bias_one = 1.0 - math.exp(1000.0 * math.log(0.9))
bias_two = 1.0 - math.exp(1000.0 * math.log(0.999))
adam_eps = 1e-08
weight_decay = 0.1

MESH = pl.DeviceIdType.MESH
NT = (((1,), (1,)), ((), ()))
NN = (((1,), (0,)), ((), ()))
TN = (((0,), (0,)), ((), ()))
RING = 8
SLOT = 32
RANK = 32
PART = 384
f32 = jnp.float32
bf16 = jnp.bfloat16


def dot(a, b, dims=NN):
    return lax.dot_general(a, b, dims, preferred_element_type=f32)


def kernel(
    tok_ref, grad_ref, chosen_ref, weight_ref, gate_ref, up_ref, down_ref, first_ref, second_ref,
    out_ref, sum_ref,
    tg, wg, wu, wd, ab, gr, shard, ms, mr, rp, rm, factor, act, slope, hid, lg,
    ag_send, ag_recv, own_send, own_recv, w_send, w_recv, rs_send, rs_recv, ab_send, ab_recv,
    gab_send, gab_recv, m_send, m_recv, own_sem,
):
    tokens, width = tok_ref.shape
    units = gate_ref.shape[1]
    half = width // 2
    eighth = width // 8
    unit_count = units // 8
    dp = lax.axis_index("dp")
    ex = lax.axis_index("expert")
    z, xh, core = ex // 4, (ex // 2) % 2, ex % 2
    y, xl = dp // 2, dp % 2

    def at(zz, hh, cc):
        return (zz * 2 + hh) * 2 + cc

    zp = (dp, at((z + 1) % RING, xh, core))
    zm = (dp, at((z + RING - 1) % RING, xh, core))
    sib = (dp, at(z, xh, 1 - core))
    cross = (y * 2 + 1 - xl, at(z, 1 - xh, core))
    xlo = (y * 2 + 1 - xl, ex)
    yp = (((y + 1) % 4) * 2 + xl, ex)
    ym = (((y + 3) % 4) * 2 + xl, ex)

    def plane(k, j):
        hh = xh if k < 2 else 1 - xh
        cc = core if k % 2 == 0 else 1 - core
        return ((dp + j) % 8, at(z, hh, cc))

    def each_peer(f):
        for k in range(4):
            lax.fori_loop(1 if k == 0 else 0, 8, functools.partial(lambda k, j, c: (f(k, j), c)[1], k), 0)

    barrier = pltpu.get_barrier_semaphore()

    def greet(device):
        pl.semaphore_signal(barrier, inc=1, device_id=device, device_id_type=MESH)

    each_peer(lambda k, j: greet(plane(k, j)))
    lax.fori_loop(1, RING, lambda r, c: (greet((dp, at((z + r) % RING, xh, core))), c)[1], 0)
    pl.semaphore_wait(barrier, 31 + RING - 1)

    def remote(src, dst, send, recv, device):
        return pltpu.make_async_remote_copy(
            src_ref=src, dst_ref=dst, send_sem=send, recv_sem=recv, device_id=device, device_id_type=MESH
        )

    def sl(r):
        return (r + 2) % RING

    def piece(ref, h):
        return ref.at[:, pl.ds(h * half, half)]

    def ag(a, way, hop, h):
        own = tok_ref if a == 0 else grad_ref
        here = hop if way == 0 else RING - hop
        there = hop + 1 if way == 0 else RING - hop - 1
        src = own if hop == 0 else tg.at[a, sl(here)]
        return remote(
            piece(src, h), piece(tg.at[a, sl(there)], h), ag_send.at[a, way, hop, h],
            ag_recv.at[a, there, h], zp if way == 0 else zm,
        )

    def ag_has(hop, way, h):
        return hop < 3 or h == way

    def ag_own(a):
        for h in range(2):
            for way in range(2):
                ag(a, way, 0, h).start()

    def ag_arrive(a, hop, h):
        for way in range(2):
            if ag_has(hop - 1, way, h):
                ag(a, way, hop - 1, h).wait_recv()
                if hop < 4 and ag_has(hop, way, h):
                    ag(a, way, hop, h).start()

    def ag_sent(a, hops):
        for hop in hops:
            for h in range(2):
                for way in range(2):
                    if ag_has(hop, way, h):
                        ag(a, way, hop, h).wait_send()

    own_w = (gate_ref.at[0], up_ref.at[0], down_ref.at[0])
    all_w = (wg, wu, wd)
    mine = (y % 2) * 2
    other = 2 - mine

    def w_copy(i, n):
        m, j = i // 2, i % 2
        quarter = (
            mine + 1 - xl, mine + xl, mine + xl, mine + 1 - xl,
            mine + xl, mine + 1 - xl, other + xl, other + 1 - xl,
        )[n]
        cols = pl.ds(pl.multiple_of((quarter * 2 + j) * eighth, eighth), eighth)
        src = own_w[m] if n == 0 else all_w[m].at[2]
        dst = all_w[m].at[2 if n < 4 else 3]
        device = (cross, xlo, ym, yp, sib, sib, sib, sib)[n]
        return remote(src.at[:, cols], dst.at[:, cols], w_send.at[i, n], w_recv.at[i, n], device)

    def w_own(m):
        return remote(own_w[m], all_w[m].at[1], own_send.at[m], own_recv.at[m], sib)

    def w_first(i):
        w_copy(i, 0).wait_recv()
        for n in (1, 2, 4):
            w_copy(i, n).start()
        if i < 4:
            w_copy(i + 2, 0).start()

    def w_second(i):
        w_copy(i, 1).wait_recv()
        for n in (3, 5):
            w_copy(i, n).start()
        w_copy(i, 2).wait_recv()
        w_copy(i, 6).start()

    def w_third(i):
        w_copy(i, 3).wait_recv()
        w_copy(i, 7).start()

    def w_have(some):
        for i in some:
            for n in (4, 5, 6, 7):
                w_copy(i, n).wait_recv()

    ag_own(0)
    w_copy(0, 0).start()
    w_copy(1, 0).start()
    own_copies = [pltpu.make_async_copy(own_w[m], all_w[m].at[0], own_sem.at[2 + m]) for m in range(3)]
    own_tok = pltpu.make_async_copy(tok_ref, tg.at[0, sl(0)], own_sem.at[0])
    own_grad = pltpu.make_async_copy(grad_ref, tg.at[1, sl(0)], own_sem.at[1])
    own_tok.start()
    own_grad.start()
    for m in range(3):
        w_own(m).start()
        own_copies[m].start()

    shard[...] = jnp.zeros_like(shard)
    shard[:, 0:unit_count] = first_ref[0].astype(bf16)
    shard[:, 128:PART] = second_ref[0].astype(bf16)
    ab[pl.ds(dp, 1)] = shard[...][None]

    def ab_copy(k, j):
        return remote(shard, ab.at[k * 8 + dp], ab_send, ab_recv, plane(k, j))

    each_peer(lambda k, j: ab_copy(k, j).start())

    ids = lax.broadcasted_iota(jnp.int32, (4 * RING, tokens), 0)
    named = jnp.zeros((4 * RING, tokens), f32)
    weighted = jnp.zeros((4 * RING, tokens), f32)
    for k in range(chosen_ref.shape[0]):
        hit = ids == chosen_ref[k : k + 1, :]
        named = jnp.where(hit, 1.0, named)
        weighted = jnp.where(hit, weight_ref[k : k + 1, :], weighted)
    earlier = lax.broadcasted_iota(jnp.int32, (tokens, tokens), 0) < lax.broadcasted_iota(
        jnp.int32, (tokens, tokens), 1
    )
    rank = dot(named.astype(bf16), jnp.where(earlier, 1.0, 0.0).astype(bf16))
    rank = jnp.where(named > 0.5, rank, -1.0)
    for zz in range(RING):
        ms[zz, 0:4, :] = rank[zz * 4 : zz * 4 + 4]
        ms[zz, 4:8, :] = weighted[zz * 4 : zz * 4 + 4]
    mr[pl.ds(sl(0), 1)] = ms[pl.ds(z, 1)]

    def m_copy(r):
        there = (z + r) % RING
        return remote(ms.at[there], mr.at[sl(r)], m_send, m_recv, (dp, at(there, xh, core)))

    lax.fori_loop(1, RING, lambda r, c: (m_copy(r).start(), c)[1], 0)

    def spread(d):
        i = lax.broadcasted_iota(jnp.int32, (128, units), 0)
        j = lax.broadcasted_iota(jnp.int32, (128, units), 1)
        return jnp.where((j - d * unit_count == i) & (i < unit_count), 1.0, 0.0).astype(bf16)

    def assemble(d, carry):
        one = spread(d)
        for k in range(4):
            factor[k] = factor[k] + dot(ab[k * 8 + d, :, 0:128], one)
        return carry

    slots = lax.broadcasted_iota(jnp.int32, (SLOT, tokens), 0).astype(f32)

    def row_of(k):
        hh = xh if k < 2 else 1 - xh
        cc = core if k % 2 == 0 else 1 - core
        return hh * 2 + cc

    def picks(b):
        return [jnp.where(slots == mr[b, pl.ds(row_of(k), 1), :], 1.0, 0.0) for k in range(4)]

    def gather_tokens(b, carry):
        tg[0, b] = dot(jnp.concatenate(picks(b), axis=0).astype(bf16), tg[0, b]).astype(bf16)
        return carry

    def gather_grads(b, carry):
        chosen = picks(b)
        scale = jnp.concatenate(
            [
                jnp.sum(chosen[k] * mr[b, pl.ds(row_of(k) + 4, 1), :], axis=1, keepdims=True)
                for k in range(4)
            ],
            axis=0,
        )
        pick = jnp.concatenate(chosen, axis=0).astype(bf16)
        tg[1, b] = (dot(pick, tg[1, b]) * scale).astype(bf16)
        return carry

    def rows_of(k):
        return pl.ds(pl.multiple_of(k * SLOT, SLOT), SLOT)

    def forward(k, carry):
        x = tg[0, :, rows_of(k), :].reshape(RING * SLOT, width)
        gate_pre = dot(x, wg[k], NT)
        up_pre = dot(x, wu[k], NT)
        s = jax.nn.sigmoid(gate_pre)
        activated = gate_pre * s
        act[k] = activated
        hid[k] = (activated * up_pre).astype(bf16)
        slope[k] = up_pre * s * (1.0 + gate_pre * (1.0 - s))
        return carry

    def second_factor(k):
        return jnp.concatenate([ab[k * 8 + d, :, 128:PART] for d in range(8)], axis=1)

    def backward(first, blocks):
        rows = slice(first * SLOT, (first + blocks) * SLOT)
        near = slice(first, first + blocks)

        def one(k, carry):
            g = tg[1, near, rows_of(k), :].reshape(blocks * SLOT, width)
            low_grad = dot(g, second_factor(k), NT).astype(bf16)
            lg[k, rows, :] = low_grad
            hidden_grad = dot(g, wd[k], NT) + adapter_scale * dot(low_grad, factor[k].astype(bf16))
            gate_grad = (hidden_grad * slope[k, rows, :]).astype(bf16)
            up_grad = (hidden_grad * act[k, rows, :]).astype(bf16)
            pair = dot(gate_grad, wg[k]) + dot(up_grad, wu[k])
            tg[0, near, rows_of(k), :] = pair.astype(bf16).reshape(blocks, SLOT, width)
            return carry

        return one

    def combine(b, carry):
        pick = jnp.concatenate(picks(b), axis=0).astype(bf16)
        tg[0, b] = dot(pick, tg[0, b], TN).astype(bf16)
        return carry

    def adapter_grads(k, carry):
        g = tg[1, :, rows_of(k), :].reshape(RING * SLOT, width)
        low_rank = dot(hid[k], factor[k].astype(bf16), NT).astype(bf16)
        grad_a = (adapter_scale * dot(lg[k], hid[k], TN)).astype(bf16)
        grad_b = (adapter_scale * dot(low_rank, g, TN)).astype(bf16)
        for d in range(8):
            ab[k * 8 + d, :, 0:128] = dot(grad_a, spread(d), NT).astype(bf16)
            ab[k * 8 + d, :, 128:PART] = grad_b[:, d * 256 : d * 256 + 256]
        return carry

    ag_arrive(0, 1, 0)
    w_first(0)
    ag_arrive(0, 1, 1)
    w_first(1)
    ag_arrive(0, 2, 0)
    w_second(0)
    w_first(2)
    ag_arrive(0, 2, 1)
    many = ab.at[pl.ds(0, 31)]
    pltpu.make_async_copy(many, many, ab_recv).wait()
    pltpu.make_async_copy(many, many, ab_send).wait()
    factor[...] = jnp.zeros_like(factor)
    lax.fori_loop(0, 4, assemble, 0)
    w_second(1)
    ag_arrive(0, 3, 0)
    ag_own(1)
    w_third(0)
    w_first(3)
    lax.fori_loop(4, 8, assemble, 0)
    ag_arrive(0, 3, 1)
    w_second(2)
    w_third(1)
    seven = mr.at[pl.ds(0, RING - 1)]
    pltpu.make_async_copy(seven, seven, m_recv).wait()
    pltpu.make_async_copy(seven, seven, m_send).wait()
    own_tok.wait()
    own_grad.wait()
    ag_arrive(0, 4, 0)
    ag_arrive(0, 4, 1)

    w_first(4)
    w_second(3)
    w_third(2)
    ag_sent(0, range(4))
    ag_arrive(1, 1, 0)
    lax.fori_loop(0, RING, gather_tokens, 0)
    for m in range(3):
        own_copies[m].wait()
        w_own(m).wait_recv()
    w_first(5)
    w_second(4)
    w_third(3)
    ag_arrive(1, 1, 1)
    lax.fori_loop(0, 2, forward, 0)
    ag_arrive(1, 2, 0)
    w_have((0, 1, 2, 3))
    w_second(5)
    w_third(4)
    lax.fori_loop(2, 4, forward, 0)
    ag_arrive(1, 2, 1)
    w_third(5)
    ag_sent(1, (1, 2))
    lax.fori_loop(0, 5, gather_grads, 0)
    ag_arrive(1, 3, 0)
    lax.fori_loop(0, 2, backward(0, 5), 0)
    ag_arrive(1, 3, 1)
    w_have((4, 5))
    lax.fori_loop(2, 4, backward(0, 5), 0)
    ag_arrive(1, 4, 0)
    ag_arrive(1, 4, 1)
    ag_sent(1, (0, 3))
    lax.fori_loop(5, RING, gather_grads, 0)
    lax.fori_loop(0, 4, backward(5, 3), 0)
    lax.fori_loop(5, RING, combine, 0)

    def landing(way, step, h):
        return (rp if way == 0 else rm).at[0 if step == 0 else 2 * step - 1 + h]

    def rs(way, step, h):
        here = 4 + step if way == 0 else 4 - step
        return remote(
            piece(tg.at[0, sl(here)], h), landing(way, step, h), rs_send.at[way, step, h],
            rs_recv.at[way, step, h], zp if way == 0 else zm,
        )

    def rs_add(way, step, h):
        rs(way, step, h).wait_recv()
        here = sl(5 + step if way == 0 else 3 - step)
        cols = slice(h * half, h * half + half)
        tg[0, here, :, cols] = (
            tg[0, here, :, cols].astype(f32) + landing(way, step, h)[...].astype(f32)
        ).astype(bf16)
        rs(way, step + 1, h).start()

    for way in range(2):
        rs(way, 0, way).start()
        rs(way, 1, 1 - way).start()
    lax.fori_loop(0, 5, combine, 0)
    for way in range(2):
        rs_add(way, 0, way)
    lax.fori_loop(0, 2, adapter_grads, 0)
    for way in range(2):
        rs_add(way, 1, 1 - way)
    lax.fori_loop(2, 4, adapter_grads, 0)

    def gab_copy(k, j):
        return remote(ab.at[k * 8 + (dp + j) % 8], gr.at[k * 8 + dp], gab_send, gab_recv, plane(k, j))

    each_peer(lambda k, j: gab_copy(k, j).start())
    for way in range(2):
        rs_add(way, 1, way)
    for way in range(2):
        rs_add(way, 2, 1 - way)
    for way in range(2):
        rs_add(way, 2, way)

    many_g = gr.at[pl.ds(0, 31)]
    pltpu.make_async_copy(many_g, many_g, gab_recv).wait()
    pltpu.make_async_copy(many_g, many_g, gab_send).wait()
    gr[pl.ds(dp, 1)] = ab[pl.ds(dp, 1)]
    sum_ref[...] = lax.fori_loop(
        0, 32, lambda i, total: total + gr[i].astype(f32), jnp.zeros((RANK, PART), f32)
    )
    for i in range(6):
        for n in range(8):
            w_copy(i, n).wait_send()
    for m in range(3):
        w_own(m).wait_send()
    for h in (1, 0):
        rs(0, 3, h).wait_recv()
        rs(1, 3, h).wait_recv()
        cols = slice(h * half, h * half + half)
        out_ref[:, cols] = (
            tg[0, sl(0), :, cols].astype(f32)
            + landing(0, 3, h)[...].astype(f32)
            + landing(1, 3, h)[...].astype(f32)
        ).astype(bf16)
    for way in range(2):
        for step in range(4):
            for h in range(2):
                if step > 0 or h == way:
                    rs(way, step, h).wait_send()


def expert_layer(tokens, grads, chosen, weights, gate, up, down, first, second):
    count, width = tokens.shape
    units = gate.shape[1]
    rows = RING * SLOT
    vmem = pl.BlockSpec(memory_space=pltpu.VMEM)
    hbm = pl.BlockSpec(memory_space=pl.ANY)
    dma = pltpu.SemaphoreType.DMA
    return pl.pallas_call(
        kernel,
        out_shape=(
            jax.ShapeDtypeStruct((count, width), bf16),
            jax.ShapeDtypeStruct((RANK, PART), f32),
        ),
        in_specs=[hbm, hbm, vmem, vmem, hbm, hbm, hbm, vmem, vmem],
        out_specs=(vmem, vmem),
        scratch_shapes=[
            pltpu.VMEM((2, RING, count, width), bf16),
            pltpu.VMEM((4, units, width), bf16),
            pltpu.VMEM((4, units, width), bf16),
            pltpu.VMEM((4, units, width), bf16),
            pltpu.VMEM((32, RANK, PART), bf16),
            pltpu.VMEM((32, RANK, PART), bf16),
            pltpu.VMEM((RANK, PART), bf16),
            pltpu.VMEM((RING, 8, count), f32),
            pltpu.VMEM((RING, 8, count), f32),
            pltpu.VMEM((7, count, width // 2), bf16),
            pltpu.VMEM((7, count, width // 2), bf16),
            pltpu.VMEM((4, RANK, units), f32),
            pltpu.VMEM((4, rows, units), f32),
            pltpu.VMEM((4, rows, units), f32),
            pltpu.VMEM((4, rows, units), bf16),
            pltpu.VMEM((4, rows, RANK), bf16),
            dma((2, 2, 4, 2)),
            dma((2, 8, 2)),
            dma((3,)),
            dma((3,)),
            dma((6, 8)),
            dma((6, 8)),
            dma((2, 4, 2)),
            dma((2, 4, 2)),
            dma,
            dma,
            dma,
            dma,
            dma,
            dma,
            dma((5,)),
        ],
        compiler_params=pltpu.CompilerParams(
            collective_id=0, has_side_effects=True, vmem_limit_bytes=60 * 1024 * 1024
        ),
        name="expert_layer",
    )(tokens, grads, chosen, weights, gate, up, down, first, second)


def decoupled_adam_update(param, grad, moment, second):
    moment_new = beta_one * moment + (1.0 - beta_one) * grad
    second_new = beta_two * second + (1.0 - beta_two) * grad * grad
    update = (
        moment_new / bias_one / (jnp.sqrt(second_new / bias_two) + adam_eps) + weight_decay * param
    )
    return (moment_new, second_new, update)


def shards(
    tokens,
    output_gradient,
    chosen_expert_index,
    router_weight,
    gate_weight,
    up_weight,
    down_weight,
    adapter_down_first,
    adapter_down_second,
    first_mean_a,
    squared_mean_a,
    first_mean_b,
    squared_mean_b,
):
    unit_count = adapter_down_first.shape[1]
    token_grad, sums = expert_layer(
        tokens,
        output_gradient,
        chosen_expert_index.T,
        router_weight.T,
        jnp.swapaxes(gate_weight, 1, 2),
        jnp.swapaxes(up_weight, 1, 2),
        down_weight,
        jnp.swapaxes(adapter_down_first, 1, 2),
        adapter_down_second,
    )
    updated_a = decoupled_adam_update(
        adapter_down_first[0], sums[:, :unit_count].T, first_mean_a[0], squared_mean_a[0]
    )
    updated_b = decoupled_adam_update(
        adapter_down_second[0], sums[:, 128:], first_mean_b[0], squared_mean_b[0]
    )
    return (token_grad, *(v[None] for v in updated_a), *(v[None] for v in updated_b))


def solution(mesh):
    rows = P(("dp", "expert"), None)
    frozen = P("expert", None, None)
    first = P("expert", "dp", None)
    second = P("expert", None, "dp")
    return jax.shard_map(
        shards,
        mesh=mesh,
        in_specs=(rows,) * 4 + (frozen,) * 3 + (first, second, first, first, second, second),
        out_specs=(rows, first, first, first, second, second, second),
        check_vma=False,
    )
```

```python
import functools
import math

import jax
import jax.numpy as jnp
from jax import lax
from jax.experimental import pallas as pl
from jax.experimental.pallas import tpu as pltpu
from jax.sharding import PartitionSpec as P

adapter_scale = 2.0
beta_one = 0.9
beta_two = 0.999
bias_one = 1.0 - math.exp(1000.0 * math.log(0.9))
bias_two = 1.0 - math.exp(1000.0 * math.log(0.999))
adam_eps = 1e-08
weight_decay = 0.1

MESH = pl.DeviceIdType.MESH
NT = (((1,), (1,)), ((), ()))
NN = (((1,), (0,)), ((), ()))
TN = (((0,), (0,)), ((), ()))
RING = 8
SLOT = 32
RANK = 32
PART = 384
f32 = jnp.float32
bf16 = jnp.bfloat16


def dot(a, b, dims=NN):
    return lax.dot_general(a, b, dims, preferred_element_type=f32)


def kernel(
    tok_ref, grad_ref, chosen_ref, weight_ref, gate_ref, up_ref, down_ref, first_ref, second_ref,
    out_ref, sum_ref,
    tg, wg, wu, wd, ab, gr, shard, ms, mr, rp, rm, factor, act, slope, hid, lg,
    ag_send, ag_recv, own_send, own_recv, w_send, w_recv, rs_send, rs_recv, ab_send, ab_recv,
    gab_send, gab_recv, m_send, m_recv, own_sem,
):
    tokens, width = tok_ref.shape
    units = gate_ref.shape[1]
    half = width // 2
    eighth = width // 8
    unit_count = units // 8
    dp = lax.axis_index("dp")
    ex = lax.axis_index("expert")
    z, xh, core = ex // 4, (ex // 2) % 2, ex % 2
    y, xl = dp // 2, dp % 2

    def at(zz, hh, cc):
        return (zz * 2 + hh) * 2 + cc

    zp = (dp, at((z + 1) % RING, xh, core))
    zm = (dp, at((z + RING - 1) % RING, xh, core))
    sib = (dp, at(z, xh, 1 - core))
    cross = (y * 2 + 1 - xl, at(z, 1 - xh, core))
    xlo = (y * 2 + 1 - xl, ex)
    yp = (((y + 1) % 4) * 2 + xl, ex)
    ym = (((y + 3) % 4) * 2 + xl, ex)

    def plane(k, j):
        hh = xh if k < 2 else 1 - xh
        cc = core if k % 2 == 0 else 1 - core
        return ((dp + j) % 8, at(z, hh, cc))

    def each_peer(f):
        for k in range(4):
            lax.fori_loop(1 if k == 0 else 0, 8, functools.partial(lambda k, j, c: (f(k, j), c)[1], k), 0)

    barrier = pltpu.get_barrier_semaphore()

    def greet(device):
        pl.semaphore_signal(barrier, inc=1, device_id=device, device_id_type=MESH)

    each_peer(lambda k, j: greet(plane(k, j)))
    lax.fori_loop(1, RING, lambda r, c: (greet((dp, at((z + r) % RING, xh, core))), c)[1], 0)
    pl.semaphore_wait(barrier, 31 + RING - 1)

    def remote(src, dst, send, recv, device):
        return pltpu.make_async_remote_copy(
            src_ref=src, dst_ref=dst, send_sem=send, recv_sem=recv, device_id=device, device_id_type=MESH
        )

    def sl(r):
        return (r + 2) % RING

    def piece(ref, h):
        return ref.at[:, pl.ds(h * half, half)]

    def ag(a, way, hop, h):
        own = tok_ref if a == 0 else grad_ref
        here = hop if way == 0 else RING - hop
        there = hop + 1 if way == 0 else RING - hop - 1
        src = own if hop == 0 else tg.at[a, sl(here)]
        return remote(
            piece(src, h), piece(tg.at[a, sl(there)], h), ag_send.at[a, way, hop, h],
            ag_recv.at[a, there, h], zp if way == 0 else zm,
        )

    def ag_has(hop, way, h):
        return hop < 3 or h == way

    def ag_own(a):
        for h in range(2):
            for way in range(2):
                ag(a, way, 0, h).start()

    def ag_arrive(a, hop, h):
        for way in range(2):
            if ag_has(hop - 1, way, h):
                ag(a, way, hop - 1, h).wait_recv()
                if hop < 4 and ag_has(hop, way, h):
                    ag(a, way, hop, h).start()

    def ag_sent(a, hops):
        for hop in hops:
            for h in range(2):
                for way in range(2):
                    if ag_has(hop, way, h):
                        ag(a, way, hop, h).wait_send()

    own_w = (gate_ref.at[0], up_ref.at[0], down_ref.at[0])
    all_w = (wg, wu, wd)
    mine = (y % 2) * 2
    other = 2 - mine

    def w_copy(i, n):
        m, j = i // 2, i % 2
        quarter = (
            mine + 1 - xl, mine + xl, mine + xl, mine + 1 - xl,
            mine + xl, mine + 1 - xl, other + xl, other + 1 - xl,
        )[n]
        cols = pl.ds(pl.multiple_of((quarter * 2 + j) * eighth, eighth), eighth)
        src = own_w[m] if n == 0 else all_w[m].at[2]
        dst = all_w[m].at[2 if n < 4 else 3]
        device = (cross, xlo, ym, yp, sib, sib, sib, sib)[n]
        return remote(src.at[:, cols], dst.at[:, cols], w_send.at[i, n], w_recv.at[i, n], device)

    def w_own(m):
        return remote(own_w[m], all_w[m].at[1], own_send.at[m], own_recv.at[m], sib)

    def w_first(i):
        w_copy(i, 0).wait_recv()
        for n in (1, 2, 4):
            w_copy(i, n).start()
        if i < 4:
            w_copy(i + 2, 0).start()

    def w_second(i):
        w_copy(i, 1).wait_recv()
        for n in (3, 5):
            w_copy(i, n).start()
        w_copy(i, 2).wait_recv()
        w_copy(i, 6).start()

    def w_third(i):
        w_copy(i, 3).wait_recv()
        w_copy(i, 7).start()

    def w_have(some):
        for i in some:
            for n in (4, 5, 6, 7):
                w_copy(i, n).wait_recv()

    ag_own(0)
    w_copy(0, 0).start()
    w_copy(1, 0).start()
    own_copies = [pltpu.make_async_copy(own_w[m], all_w[m].at[0], own_sem.at[2 + m]) for m in range(3)]
    own_tok = pltpu.make_async_copy(tok_ref, tg.at[0, sl(0)], own_sem.at[0])
    own_grad = pltpu.make_async_copy(grad_ref, tg.at[1, sl(0)], own_sem.at[1])
    own_tok.start()
    own_grad.start()
    for m in range(3):
        w_own(m).start()
        own_copies[m].start()

    shard[...] = jnp.zeros_like(shard)
    shard[:, 0:unit_count] = first_ref[0].astype(bf16)
    shard[:, 128:PART] = second_ref[0].astype(bf16)
    ab[pl.ds(dp, 1)] = shard[...][None]

    def ab_copy(k, j):
        return remote(shard, ab.at[k * 8 + dp], ab_send, ab_recv, plane(k, j))


    ids = lax.broadcasted_iota(jnp.int32, (4 * RING, tokens), 0)
    named = jnp.zeros((4 * RING, tokens), f32)
    weighted = jnp.zeros((4 * RING, tokens), f32)
    for k in range(chosen_ref.shape[0]):
        hit = ids == chosen_ref[k : k + 1, :]
        named = jnp.where(hit, 1.0, named)
        weighted = jnp.where(hit, weight_ref[k : k + 1, :], weighted)
    earlier = lax.broadcasted_iota(jnp.int32, (tokens, tokens), 0) < lax.broadcasted_iota(
        jnp.int32, (tokens, tokens), 1
    )
    rank = dot(named.astype(bf16), jnp.where(earlier, 1.0, 0.0).astype(bf16))
    rank = jnp.where(named > 0.5, rank, -1.0)
    for zz in range(RING):
        ms[zz, 0:4, :] = rank[zz * 4 : zz * 4 + 4]
        ms[zz, 4:8, :] = weighted[zz * 4 : zz * 4 + 4]
    mr[pl.ds(sl(0), 1)] = ms[pl.ds(z, 1)]

    def m_copy(r):
        there = (z + r) % RING
        return remote(ms.at[there], mr.at[sl(r)], m_send, m_recv, (dp, at(there, xh, core)))

    lax.fori_loop(1, RING, lambda r, c: (m_copy(r).start(), c)[1], 0)

    def spread(d):
        i = lax.broadcasted_iota(jnp.int32, (128, units), 0)
        j = lax.broadcasted_iota(jnp.int32, (128, units), 1)
        return jnp.where((j - d * unit_count == i) & (i < unit_count), 1.0, 0.0).astype(bf16)

    def assemble(d, carry):
        one = spread(d)
        for k in range(4):
            factor[k] = factor[k] + dot(ab[k * 8 + d, :, 0:128], one)
        return carry

    slots = lax.broadcasted_iota(jnp.int32, (SLOT, tokens), 0).astype(f32)

    def row_of(k):
        hh = xh if k < 2 else 1 - xh
        cc = core if k % 2 == 0 else 1 - core
        return hh * 2 + cc

    def picks(b):
        return [jnp.where(slots == mr[b, pl.ds(row_of(k), 1), :], 1.0, 0.0) for k in range(4)]

    def gather_tokens(b, carry):
        tg[0, b] = dot(jnp.concatenate(picks(b), axis=0).astype(bf16), tg[0, b]).astype(bf16)
        return carry

    def gather_grads(b, carry):
        chosen = picks(b)
        scale = jnp.concatenate(
            [
                jnp.sum(chosen[k] * mr[b, pl.ds(row_of(k) + 4, 1), :], axis=1, keepdims=True)
                for k in range(4)
            ],
            axis=0,
        )
        pick = jnp.concatenate(chosen, axis=0).astype(bf16)
        tg[1, b] = (dot(pick, tg[1, b]) * scale).astype(bf16)
        return carry

    def rows_of(k):
        return pl.ds(pl.multiple_of(k * SLOT, SLOT), SLOT)

    def forward(k, carry):
        x = tg[0, :, rows_of(k), :].reshape(RING * SLOT, width)
        gate_pre = dot(x, wg[k], NT)
        up_pre = dot(x, wu[k], NT)
        s = jax.nn.sigmoid(gate_pre)
        activated = gate_pre * s
        act[k] = activated
        hid[k] = (activated * up_pre).astype(bf16)
        slope[k] = up_pre * s * (1.0 + gate_pre * (1.0 - s))
        return carry

    def second_factor(k):
        return jnp.concatenate([ab[k * 8 + d, :, 128:PART] for d in range(8)], axis=1)

    def backward(first, blocks):
        rows = slice(first * SLOT, (first + blocks) * SLOT)
        near = slice(first, first + blocks)

        def one(k, carry):
            g = tg[1, near, rows_of(k), :].reshape(blocks * SLOT, width)
            low_grad = dot(g, second_factor(k), NT).astype(bf16)
            lg[k, rows, :] = low_grad
            hidden_grad = dot(g, wd[k], NT) + adapter_scale * dot(low_grad, factor[k].astype(bf16))
            gate_grad = (hidden_grad * slope[k, rows, :]).astype(bf16)
            up_grad = (hidden_grad * act[k, rows, :]).astype(bf16)
            pair = dot(gate_grad, wg[k]) + dot(up_grad, wu[k])
            tg[0, near, rows_of(k), :] = pair.astype(bf16).reshape(blocks, SLOT, width)
            return carry

        return one

    far = slice(5 * SLOT, RING * SLOT)

    def far_slopes(k, carry):
        g = tg[1, 5:RING, rows_of(k), :].reshape(3 * SLOT, width)
        low_grad = dot(g, second_factor(k), NT).astype(bf16)
        lg[k, far, :] = low_grad
        hidden_grad = dot(g, wd[k], NT) + adapter_scale * dot(low_grad, factor[k].astype(bf16))
        slope[k, far, :] = (hidden_grad * slope[k, far, :]).astype(bf16).astype(f32)
        act[k, far, :] = (hidden_grad * act[k, far, :]).astype(bf16).astype(f32)
        return carry

    def far_pairs(h):
        cols = slice(h * half, h * half + half)

        def one(k, carry):
            pair = dot(slope[k, far, :].astype(bf16), wg[k, :, cols]) + dot(
                act[k, far, :].astype(bf16), wu[k, :, cols]
            )
            tg[0, 5:RING, rows_of(k), cols] = pair.astype(bf16).reshape(3, SLOT, half)
            return carry

        def sums(b, carry):
            pick = jnp.concatenate(picks(b), axis=0).astype(bf16)
            tg[0, b, :, cols] = dot(pick, tg[0, b, :, cols], TN).astype(bf16)
            return carry

        lax.fori_loop(0, 4, one, 0)
        lax.fori_loop(5, RING, sums, 0)

    def combine(b, carry):
        pick = jnp.concatenate(picks(b), axis=0).astype(bf16)
        tg[0, b] = dot(pick, tg[0, b], TN).astype(bf16)
        return carry

    def adapter_grads(k, carry):
        g = tg[1, :, rows_of(k), :].reshape(RING * SLOT, width)
        low_rank = dot(hid[k], factor[k].astype(bf16), NT).astype(bf16)
        grad_a = (adapter_scale * dot(lg[k], hid[k], TN)).astype(bf16)
        grad_b = (adapter_scale * dot(low_rank, g, TN)).astype(bf16)
        for d in range(8):
            ab[k * 8 + d, :, 0:128] = dot(grad_a, spread(d), NT).astype(bf16)
            ab[k * 8 + d, :, 128:PART] = grad_b[:, d * 256 : d * 256 + 256]
        return carry

    ag_arrive(0, 1, 0)
    w_first(0)
    ag_arrive(0, 1, 1)
    w_first(1)
    ag_arrive(0, 2, 0)
    w_second(0)
    ag_arrive(0, 2, 1)
    w_first(2)
    each_peer(lambda k, j: ab_copy(k, j).start())
    w_second(1)
    ag_arrive(0, 3, 0)
    w_third(0)
    ag_arrive(0, 3, 1)
    ag_own(1)
    w_first(3)
    w_second(2)
    own_tok.wait()
    own_grad.wait()
    seven = mr.at[pl.ds(0, RING - 1)]
    pltpu.make_async_copy(seven, seven, m_recv).wait()
    pltpu.make_async_copy(seven, seven, m_send).wait()
    ag_arrive(0, 4, 0)
    ag_arrive(0, 4, 1)

    w_third(1)
    w_first(4)
    w_second(3)
    ag_sent(0, range(4))
    ag_arrive(1, 1, 0)
    w_third(2)
    lax.fori_loop(0, RING, gather_tokens, 0)
    w_first(5)
    ag_arrive(1, 1, 1)
    for m in range(3):
        own_copies[m].wait()
        w_own(m).wait_recv()
    lax.fori_loop(0, 2, forward, 0)
    w_second(4)
    w_third(3)
    ag_arrive(1, 2, 0)
    w_have((0, 1, 2, 3))
    lax.fori_loop(2, 4, forward, 0)
    w_second(5)
    w_third(4)
    ag_arrive(1, 2, 1)
    many = ab.at[pl.ds(0, 31)]
    pltpu.make_async_copy(many, many, ab_recv).wait()
    pltpu.make_async_copy(many, many, ab_send).wait()
    factor[...] = jnp.zeros_like(factor)
    lax.fori_loop(0, 8, assemble, 0)
    ag_sent(1, (1, 2))
    lax.fori_loop(0, 5, gather_grads, 0)
    w_third(5)
    ag_arrive(1, 3, 0)
    lax.fori_loop(0, 2, backward(0, 5), 0)
    ag_arrive(1, 3, 1)
    w_have((4, 5))
    lax.fori_loop(2, 4, backward(0, 5), 0)
    ag_arrive(1, 4, 0)
    ag_arrive(1, 4, 1)
    ag_sent(1, (0, 3))
    lax.fori_loop(5, RING, gather_grads, 0)
    lax.fori_loop(0, 4, far_slopes, 0)

    def landing(way, step, h):
        return (rp if way == 0 else rm).at[0 if step == 0 else 2 * step - 1 + h]

    def rs(way, step, h):
        here = 4 + step if way == 0 else 4 - step
        return remote(
            piece(tg.at[0, sl(here)], h), landing(way, step, h), rs_send.at[way, step, h],
            rs_recv.at[way, step, h], zp if way == 0 else zm,
        )

    def rs_add(way, step, h):
        rs(way, step, h).wait_recv()
        here = sl(5 + step if way == 0 else 3 - step)
        cols = slice(h * half, h * half + half)
        tg[0, here, :, cols] = (
            tg[0, here, :, cols].astype(f32) + landing(way, step, h)[...].astype(f32)
        ).astype(bf16)
        rs(way, step + 1, h).start()

    for h in range(2):
        far_pairs(h)
        rs(h, 0, h).start()
        rs(1 - h, 1, h).start()
    lax.fori_loop(0, 5, combine, 0)
    for way in range(2):
        rs_add(way, 0, way)
    lax.fori_loop(0, 2, adapter_grads, 0)
    for way in range(2):
        rs_add(way, 1, 1 - way)
    lax.fori_loop(2, 4, adapter_grads, 0)

    def gab_copy(k, j):
        return remote(ab.at[k * 8 + (dp + j) % 8], gr.at[k * 8 + dp], gab_send, gab_recv, plane(k, j))

    each_peer(lambda k, j: gab_copy(k, j).start())
    for way in range(2):
        rs_add(way, 1, way)
    for way in range(2):
        rs_add(way, 2, 1 - way)
    for way in range(2):
        rs_add(way, 2, way)

    many_g = gr.at[pl.ds(0, 31)]
    pltpu.make_async_copy(many_g, many_g, gab_recv).wait()
    pltpu.make_async_copy(many_g, many_g, gab_send).wait()
    gr[pl.ds(dp, 1)] = ab[pl.ds(dp, 1)]
    sum_ref[...] = lax.fori_loop(
        0, 32, lambda i, total: total + gr[i].astype(f32), jnp.zeros((RANK, PART), f32)
    )
    for i in range(6):
        for n in range(8):
            w_copy(i, n).wait_send()
    for m in range(3):
        w_own(m).wait_send()
    for h in (1, 0):
        rs(0, 3, h).wait_recv()
        rs(1, 3, h).wait_recv()
        cols = slice(h * half, h * half + half)
        out_ref[:, cols] = (
            tg[0, sl(0), :, cols].astype(f32)
            + landing(0, 3, h)[...].astype(f32)
            + landing(1, 3, h)[...].astype(f32)
        ).astype(bf16)
    for way in range(2):
        for step in range(4):
            for h in range(2):
                if step > 0 or h == way:
                    rs(way, step, h).wait_send()


def expert_layer(tokens, grads, chosen, weights, gate, up, down, first, second):
    count, width = tokens.shape
    units = gate.shape[1]
    rows = RING * SLOT
    vmem = pl.BlockSpec(memory_space=pltpu.VMEM)
    hbm = pl.BlockSpec(memory_space=pl.ANY)
    dma = pltpu.SemaphoreType.DMA
    return pl.pallas_call(
        kernel,
        out_shape=(
            jax.ShapeDtypeStruct((count, width), bf16),
            jax.ShapeDtypeStruct((RANK, PART), f32),
        ),
        in_specs=[hbm, hbm, vmem, vmem, hbm, hbm, hbm, vmem, vmem],
        out_specs=(vmem, vmem),
        scratch_shapes=[
            pltpu.VMEM((2, RING, count, width), bf16),
            pltpu.VMEM((4, units, width), bf16),
            pltpu.VMEM((4, units, width), bf16),
            pltpu.VMEM((4, units, width), bf16),
            pltpu.VMEM((32, RANK, PART), bf16),
            pltpu.VMEM((32, RANK, PART), bf16),
            pltpu.VMEM((RANK, PART), bf16),
            pltpu.VMEM((RING, 8, count), f32),
            pltpu.VMEM((RING, 8, count), f32),
            pltpu.VMEM((7, count, width // 2), bf16),
            pltpu.VMEM((7, count, width // 2), bf16),
            pltpu.VMEM((4, RANK, units), f32),
            pltpu.VMEM((4, rows, units), f32),
            pltpu.VMEM((4, rows, units), f32),
            pltpu.VMEM((4, rows, units), bf16),
            pltpu.VMEM((4, rows, RANK), bf16),
            dma((2, 2, 4, 2)),
            dma((2, 8, 2)),
            dma((3,)),
            dma((3,)),
            dma((6, 8)),
            dma((6, 8)),
            dma((2, 4, 2)),
            dma((2, 4, 2)),
            dma,
            dma,
            dma,
            dma,
            dma,
            dma,
            dma((5,)),
        ],
        compiler_params=pltpu.CompilerParams(
            collective_id=0, has_side_effects=True, vmem_limit_bytes=60 * 1024 * 1024
        ),
        name="expert_layer",
    )(tokens, grads, chosen, weights, gate, up, down, first, second)


def decoupled_adam_update(param, grad, moment, second):
    moment_new = beta_one * moment + (1.0 - beta_one) * grad
    second_new = beta_two * second + (1.0 - beta_two) * grad * grad
    update = (
        moment_new / bias_one / (jnp.sqrt(second_new / bias_two) + adam_eps) + weight_decay * param
    )
    return (moment_new, second_new, update)


def shards(
    tokens,
    output_gradient,
    chosen_expert_index,
    router_weight,
    gate_weight,
    up_weight,
    down_weight,
    adapter_down_first,
    adapter_down_second,
    first_mean_a,
    squared_mean_a,
    first_mean_b,
    squared_mean_b,
):
    unit_count = adapter_down_first.shape[1]
    token_grad, sums = expert_layer(
        tokens,
        output_gradient,
        chosen_expert_index.T,
        router_weight.T,
        jnp.swapaxes(gate_weight, 1, 2),
        jnp.swapaxes(up_weight, 1, 2),
        down_weight,
        jnp.swapaxes(adapter_down_first, 1, 2),
        adapter_down_second,
    )
    updated_a = decoupled_adam_update(
        adapter_down_first[0], sums[:, :unit_count].T, first_mean_a[0], squared_mean_a[0]
    )
    updated_b = decoupled_adam_update(
        adapter_down_second[0], sums[:, 128:], first_mean_b[0], squared_mean_b[0]
    )
    return (token_grad, *(v[None] for v in updated_a), *(v[None] for v in updated_b))


def solution(mesh):
    rows = P(("dp", "expert"), None)
    frozen = P("expert", None, None)
    first = P("expert", "dp", None)
    second = P("expert", None, "dp")
    return jax.shard_map(
        shards,
        mesh=mesh,
        in_specs=(rows,) * 4 + (frozen,) * 3 + (first, second, first, first, second, second),
        out_specs=(rows, first, first, first, second, second, second),
        check_vma=False,
    )
```

```python
import functools
import math

import jax
import jax.numpy as jnp
from jax import lax
from jax.experimental import pallas as pl
from jax.experimental.pallas import tpu as pltpu
from jax.sharding import PartitionSpec as P

adapter_scale = 2.0
beta_one = 0.9
beta_two = 0.999
bias_one = 1.0 - math.exp(1000.0 * math.log(0.9))
bias_two = 1.0 - math.exp(1000.0 * math.log(0.999))
adam_eps = 1e-08
weight_decay = 0.1

MESH = pl.DeviceIdType.MESH
NT = (((1,), (1,)), ((), ()))
NN = (((1,), (0,)), ((), ()))
TN = (((0,), (0,)), ((), ()))
RING = 8
SLOT = 32
RANK = 32
PART = 384
f32 = jnp.float32
bf16 = jnp.bfloat16


def dot(a, b, dims=NN):
    return lax.dot_general(a, b, dims, preferred_element_type=f32)


def kernel(
    tok_ref, grad_ref, chosen_ref, weight_ref, gate_ref, up_ref, down_ref, first_ref, second_ref,
    out_ref, sum_ref,
    tg, wg, wu, wd, ab, gr, shard, ms, mr, rp, rm, factor, act, slope, hid, lg,
    ag_send, ag_recv, own_send, own_recv, w_send, w_recv, rs_send, rs_recv, ab_send, ab_recv,
    gab_send, gab_recv, m_send, m_recv, own_sem,
):
    tokens, width = tok_ref.shape
    units = gate_ref.shape[1]
    half = width // 2
    eighth = width // 8
    unit_count = units // 8
    dp = lax.axis_index("dp")
    ex = lax.axis_index("expert")
    z, xh, core = ex // 4, (ex // 2) % 2, ex % 2
    y, xl = dp // 2, dp % 2

    def at(zz, hh, cc):
        return (zz * 2 + hh) * 2 + cc

    zp = (dp, at((z + 1) % RING, xh, core))
    zm = (dp, at((z + RING - 1) % RING, xh, core))
    sib = (dp, at(z, xh, 1 - core))
    cross = (y * 2 + 1 - xl, at(z, 1 - xh, core))
    xlo = (y * 2 + 1 - xl, ex)
    yp = (((y + 1) % 4) * 2 + xl, ex)
    ym = (((y + 3) % 4) * 2 + xl, ex)

    def plane(k, j):
        hh = xh if k < 2 else 1 - xh
        cc = core if k % 2 == 0 else 1 - core
        return ((dp + j) % 8, at(z, hh, cc))

    def each_peer(f):
        for k in range(4):
            lax.fori_loop(1 if k == 0 else 0, 8, functools.partial(lambda k, j, c: (f(k, j), c)[1], k), 0)

    barrier = pltpu.get_barrier_semaphore()

    def greet(device):
        pl.semaphore_signal(barrier, inc=1, device_id=device, device_id_type=MESH)

    each_peer(lambda k, j: greet(plane(k, j)))
    lax.fori_loop(1, RING, lambda r, c: (greet((dp, at((z + r) % RING, xh, core))), c)[1], 0)
    pl.semaphore_wait(barrier, 31 + RING - 1)

    def remote(src, dst, send, recv, device):
        return pltpu.make_async_remote_copy(
            src_ref=src, dst_ref=dst, send_sem=send, recv_sem=recv, device_id=device, device_id_type=MESH
        )

    def sl(r):
        return (r + 2) % RING

    def piece(ref, h):
        return ref.at[:, pl.ds(h * half, half)]

    def ag(a, way, hop, h):
        own = tok_ref if a == 0 else grad_ref
        here = hop if way == 0 else RING - hop
        there = hop + 1 if way == 0 else RING - hop - 1
        src = own if hop == 0 else tg.at[a, sl(here)]
        return remote(
            piece(src, h), piece(tg.at[a, sl(there)], h), ag_send.at[a, way, hop, h],
            ag_recv.at[a, there, h], zp if way == 0 else zm,
        )

    def ag_has(hop, way, h):
        return hop < 3 or h == way

    def ag_own(a):
        for h in range(2):
            for way in range(2):
                ag(a, way, 0, h).start()

    def ag_arrive(a, hop, h):
        for way in range(2):
            if ag_has(hop - 1, way, h):
                ag(a, way, hop - 1, h).wait_recv()
                if hop < 4 and ag_has(hop, way, h):
                    ag(a, way, hop, h).start()

    def ag_sent(a, hops):
        for hop in hops:
            for h in range(2):
                for way in range(2):
                    if ag_has(hop, way, h):
                        ag(a, way, hop, h).wait_send()

    own_w = (gate_ref.at[0], up_ref.at[0], down_ref.at[0])
    all_w = (wg, wu, wd)
    mine = (y % 2) * 2
    other = 2 - mine

    def w_copy(i, n):
        m, j = i // 2, i % 2
        quarter = (
            mine + 1 - xl, mine + xl, mine + xl, mine + 1 - xl,
            mine + xl, mine + 1 - xl, other + xl, other + 1 - xl,
        )[n]
        cols = pl.ds(pl.multiple_of((quarter * 2 + j) * eighth, eighth), eighth)
        src = own_w[m] if n == 0 else all_w[m].at[2]
        dst = all_w[m].at[2 if n < 4 else 3]
        device = (cross, xlo, ym, yp, sib, sib, sib, sib)[n]
        return remote(src.at[:, cols], dst.at[:, cols], w_send.at[i, n], w_recv.at[i, n], device)

    def w_own(m):
        return remote(own_w[m], all_w[m].at[1], own_send.at[m], own_recv.at[m], sib)

    def w_first(i):
        w_copy(i, 0).wait_recv()
        for n in (1, 2, 4):
            w_copy(i, n).start()
        if i < 4:
            w_copy(i + 2, 0).start()

    def w_second(i):
        w_copy(i, 1).wait_recv()
        for n in (3, 5):
            w_copy(i, n).start()
        w_copy(i, 2).wait_recv()
        w_copy(i, 6).start()

    def w_third(i):
        w_copy(i, 3).wait_recv()
        w_copy(i, 7).start()

    def w_have(some):
        for i in some:
            for n in (4, 5, 6, 7):
                w_copy(i, n).wait_recv()

    ag_own(0)
    w_copy(0, 0).start()
    w_copy(1, 0).start()
    own_copies = [pltpu.make_async_copy(own_w[m], all_w[m].at[0], own_sem.at[2 + m]) for m in range(3)]
    own_tok = pltpu.make_async_copy(tok_ref, tg.at[0, sl(0)], own_sem.at[0])
    own_grad = pltpu.make_async_copy(grad_ref, tg.at[1, sl(0)], own_sem.at[1])
    own_tok.start()
    own_grad.start()
    for m in range(3):
        w_own(m).start()
        own_copies[m].start()

    shard[...] = jnp.zeros_like(shard)
    shard[:, 0:unit_count] = first_ref[0].astype(bf16)
    shard[:, 128:PART] = second_ref[0].astype(bf16)
    ab[pl.ds(dp, 1)] = shard[...][None]

    def ab_copy(k, j):
        return remote(shard, ab.at[k * 8 + dp], ab_send, ab_recv, plane(k, j))


    ids = lax.broadcasted_iota(jnp.int32, (4 * RING, tokens), 0)
    named = jnp.zeros((4 * RING, tokens), f32)
    weighted = jnp.zeros((4 * RING, tokens), f32)
    for k in range(chosen_ref.shape[0]):
        hit = ids == chosen_ref[k : k + 1, :]
        named = jnp.where(hit, 1.0, named)
        weighted = jnp.where(hit, weight_ref[k : k + 1, :], weighted)
    earlier = lax.broadcasted_iota(jnp.int32, (tokens, tokens), 0) < lax.broadcasted_iota(
        jnp.int32, (tokens, tokens), 1
    )
    rank = dot(named.astype(bf16), jnp.where(earlier, 1.0, 0.0).astype(bf16))
    rank = jnp.where(named > 0.5, rank, -1.0)
    for zz in range(RING):
        ms[zz, 0:4, :] = rank[zz * 4 : zz * 4 + 4]
        ms[zz, 4:8, :] = weighted[zz * 4 : zz * 4 + 4]
    mr[pl.ds(sl(0), 1)] = ms[pl.ds(z, 1)]

    def m_copy(r):
        there = (z + r) % RING
        return remote(ms.at[there], mr.at[sl(r)], m_send, m_recv, (dp, at(there, xh, core)))

    lax.fori_loop(1, RING, lambda r, c: (m_copy(r).start(), c)[1], 0)

    def spread(d):
        i = lax.broadcasted_iota(jnp.int32, (128, units), 0)
        j = lax.broadcasted_iota(jnp.int32, (128, units), 1)
        return jnp.where((j - d * unit_count == i) & (i < unit_count), 1.0, 0.0).astype(bf16)

    def assemble(d, carry):
        one = spread(d)
        for k in range(4):
            factor[k] = factor[k] + dot(ab[k * 8 + d, :, 0:128], one)
        return carry

    slots = lax.broadcasted_iota(jnp.int32, (SLOT, tokens), 0).astype(f32)

    def row_of(k):
        hh = xh if k < 2 else 1 - xh
        cc = core if k % 2 == 0 else 1 - core
        return hh * 2 + cc

    def picks(b):
        return [jnp.where(slots == mr[b, pl.ds(row_of(k), 1), :], 1.0, 0.0) for k in range(4)]

    def gather_tokens(b, carry):
        tg[0, b] = dot(jnp.concatenate(picks(b), axis=0).astype(bf16), tg[0, b]).astype(bf16)
        return carry

    def gather_grads(b, carry):
        chosen = picks(b)
        scale = jnp.concatenate(
            [
                jnp.sum(chosen[k] * mr[b, pl.ds(row_of(k) + 4, 1), :], axis=1, keepdims=True)
                for k in range(4)
            ],
            axis=0,
        )
        pick = jnp.concatenate(chosen, axis=0).astype(bf16)
        tg[1, b] = (dot(pick, tg[1, b]) * scale).astype(bf16)
        return carry

    def over(begin, end, f):
        for k in range(begin, end):
            f(k, 0)

    def rows_of(k):
        if isinstance(k, int):
            return slice(k * SLOT, (k + 1) * SLOT)
        return pl.ds(pl.multiple_of(k * SLOT, SLOT), SLOT)

    def forward(k, carry):
        x = tg[0, :, rows_of(k), :].reshape(RING * SLOT, width)
        gate_pre = dot(x, wg[k], NT)
        up_pre = dot(x, wu[k], NT)
        s = jax.nn.sigmoid(gate_pre)
        activated = gate_pre * s
        act[k] = activated
        hid[k] = (activated * up_pre).astype(bf16)
        slope[k] = up_pre * s * (1.0 + gate_pre * (1.0 - s))
        return carry

    def second_factor(k):
        return jnp.concatenate([ab[k * 8 + d, :, 128:PART] for d in range(8)], axis=1)

    def backward(first, blocks):
        rows = slice(first * SLOT, (first + blocks) * SLOT)
        near = slice(first, first + blocks)

        def one(k, carry):
            g = tg[1, near, rows_of(k), :].reshape(blocks * SLOT, width)
            low_grad = dot(g, second_factor(k), NT).astype(bf16)
            lg[k, rows, :] = low_grad
            hidden_grad = dot(g, wd[k], NT) + adapter_scale * dot(low_grad, factor[k].astype(bf16))
            gate_grad = (hidden_grad * slope[k, rows, :]).astype(bf16)
            up_grad = (hidden_grad * act[k, rows, :]).astype(bf16)
            pair = dot(gate_grad, wg[k]) + dot(up_grad, wu[k])
            tg[0, near, rows_of(k), :] = pair.astype(bf16).reshape(blocks, SLOT, width)
            return carry

        return one

    far = slice(5 * SLOT, RING * SLOT)

    def far_slopes(k, carry):
        g = tg[1, 5:RING, rows_of(k), :].reshape(3 * SLOT, width)
        low_grad = dot(g, second_factor(k), NT).astype(bf16)
        lg[k, far, :] = low_grad
        hidden_grad = dot(g, wd[k], NT) + adapter_scale * dot(low_grad, factor[k].astype(bf16))
        slope[k, far, :] = (hidden_grad * slope[k, far, :]).astype(bf16).astype(f32)
        act[k, far, :] = (hidden_grad * act[k, far, :]).astype(bf16).astype(f32)
        return carry

    def far_pairs(h):
        cols = slice(h * half, h * half + half)

        def one(k, carry):
            pair = dot(slope[k, far, :].astype(bf16), wg[k, :, cols]) + dot(
                act[k, far, :].astype(bf16), wu[k, :, cols]
            )
            tg[0, 5:RING, rows_of(k), cols] = pair.astype(bf16).reshape(3, SLOT, half)
            return carry

        def sums(b, carry):
            pick = jnp.concatenate(picks(b), axis=0).astype(bf16)
            tg[0, b, :, cols] = dot(pick, tg[0, b, :, cols], TN).astype(bf16)
            return carry

        over(0, 4, one)
        over(5, RING, sums)

    def combine(b, carry):
        pick = jnp.concatenate(picks(b), axis=0).astype(bf16)
        tg[0, b] = dot(pick, tg[0, b], TN).astype(bf16)
        return carry

    def adapter_grads(k, carry):
        g = tg[1, :, rows_of(k), :].reshape(RING * SLOT, width)
        low_rank = dot(hid[k], factor[k].astype(bf16), NT).astype(bf16)
        grad_a = (adapter_scale * dot(lg[k], hid[k], TN)).astype(bf16)
        grad_b = (adapter_scale * dot(low_rank, g, TN)).astype(bf16)
        for d in range(8):
            ab[k * 8 + d, :, 0:128] = dot(grad_a, spread(d), NT).astype(bf16)
            ab[k * 8 + d, :, 128:PART] = grad_b[:, d * 256 : d * 256 + 256]
        return carry

    ag_arrive(0, 1, 0)
    w_first(0)
    ag_arrive(0, 1, 1)
    w_first(1)
    ag_arrive(0, 2, 0)
    w_second(0)
    ag_arrive(0, 2, 1)
    w_first(2)
    each_peer(lambda k, j: ab_copy(k, j).start())
    w_second(1)
    ag_arrive(0, 3, 0)
    w_third(0)
    ag_arrive(0, 3, 1)
    ag_own(1)
    w_first(3)
    w_second(2)
    own_tok.wait()
    own_grad.wait()
    seven = mr.at[pl.ds(0, RING - 1)]
    pltpu.make_async_copy(seven, seven, m_recv).wait()
    pltpu.make_async_copy(seven, seven, m_send).wait()
    ag_arrive(0, 4, 0)
    ag_arrive(0, 4, 1)

    w_third(1)
    w_first(4)
    w_second(3)
    ag_sent(0, range(4))
    ag_arrive(1, 1, 0)
    w_third(2)
    lax.fori_loop(0, RING, gather_tokens, 0)
    w_first(5)
    ag_arrive(1, 1, 1)
    for m in range(3):
        own_copies[m].wait()
        w_own(m).wait_recv()
    over(0, 2, forward)
    w_second(4)
    w_third(3)
    ag_arrive(1, 2, 0)
    w_have((0, 1, 2, 3))
    over(2, 4, forward)
    w_second(5)
    w_third(4)
    ag_arrive(1, 2, 1)
    many = ab.at[pl.ds(0, 31)]
    pltpu.make_async_copy(many, many, ab_recv).wait()
    pltpu.make_async_copy(many, many, ab_send).wait()
    factor[...] = jnp.zeros_like(factor)
    lax.fori_loop(0, 8, assemble, 0)
    ag_sent(1, (1, 2))
    lax.fori_loop(0, 5, gather_grads, 0)
    w_third(5)
    ag_arrive(1, 3, 0)
    over(0, 2, backward(0, 5))
    ag_arrive(1, 3, 1)
    w_have((4, 5))
    over(2, 4, backward(0, 5))
    ag_arrive(1, 4, 0)
    ag_arrive(1, 4, 1)
    ag_sent(1, (0, 3))
    over(5, RING, gather_grads)
    over(0, 4, far_slopes)

    def landing(way, step, h):
        return (rp if way == 0 else rm).at[0 if step == 0 else 2 * step - 1 + h]

    def rs(way, step, h):
        here = 4 + step if way == 0 else 4 - step
        return remote(
            piece(tg.at[0, sl(here)], h), landing(way, step, h), rs_send.at[way, step, h],
            rs_recv.at[way, step, h], zp if way == 0 else zm,
        )

    def rs_add(way, step, h):
        rs(way, step, h).wait_recv()
        here = sl(5 + step if way == 0 else 3 - step)
        cols = slice(h * half, h * half + half)
        tg[0, here, :, cols] = (
            tg[0, here, :, cols].astype(f32) + landing(way, step, h)[...].astype(f32)
        ).astype(bf16)
        rs(way, step + 1, h).start()

    for h in range(2):
        far_pairs(h)
        rs(h, 0, h).start()
        rs(1 - h, 1, h).start()
    lax.fori_loop(0, 5, combine, 0)
    for way in range(2):
        rs_add(way, 0, way)
    lax.fori_loop(0, 2, adapter_grads, 0)
    for way in range(2):
        rs_add(way, 1, 1 - way)
    lax.fori_loop(2, 4, adapter_grads, 0)

    def gab_copy(k, j):
        return remote(ab.at[k * 8 + (dp + j) % 8], gr.at[k * 8 + dp], gab_send, gab_recv, plane(k, j))

    each_peer(lambda k, j: gab_copy(k, j).start())
    for way in range(2):
        rs_add(way, 1, way)
    for way in range(2):
        rs_add(way, 2, 1 - way)
    for way in range(2):
        rs_add(way, 2, way)

    many_g = gr.at[pl.ds(0, 31)]
    pltpu.make_async_copy(many_g, many_g, gab_recv).wait()
    pltpu.make_async_copy(many_g, many_g, gab_send).wait()
    gr[pl.ds(dp, 1)] = ab[pl.ds(dp, 1)]
    sum_ref[...] = lax.fori_loop(
        0, 32, lambda i, total: total + gr[i].astype(f32), jnp.zeros((RANK, PART), f32)
    )
    for i in range(6):
        for n in range(8):
            w_copy(i, n).wait_send()
    for m in range(3):
        w_own(m).wait_send()
    for h in (1, 0):
        rs(0, 3, h).wait_recv()
        rs(1, 3, h).wait_recv()
        cols = slice(h * half, h * half + half)
        out_ref[:, cols] = (
            tg[0, sl(0), :, cols].astype(f32)
            + landing(0, 3, h)[...].astype(f32)
            + landing(1, 3, h)[...].astype(f32)
        ).astype(bf16)
    for way in range(2):
        for step in range(4):
            for h in range(2):
                if step > 0 or h == way:
                    rs(way, step, h).wait_send()


def expert_layer(tokens, grads, chosen, weights, gate, up, down, first, second):
    count, width = tokens.shape
    units = gate.shape[1]
    rows = RING * SLOT
    vmem = pl.BlockSpec(memory_space=pltpu.VMEM)
    hbm = pl.BlockSpec(memory_space=pl.ANY)
    dma = pltpu.SemaphoreType.DMA
    return pl.pallas_call(
        kernel,
        out_shape=(
            jax.ShapeDtypeStruct((count, width), bf16),
            jax.ShapeDtypeStruct((RANK, PART), f32),
        ),
        in_specs=[hbm, hbm, vmem, vmem, hbm, hbm, hbm, vmem, vmem],
        out_specs=(vmem, vmem),
        scratch_shapes=[
            pltpu.VMEM((2, RING, count, width), bf16),
            pltpu.VMEM((4, units, width), bf16),
            pltpu.VMEM((4, units, width), bf16),
            pltpu.VMEM((4, units, width), bf16),
            pltpu.VMEM((32, RANK, PART), bf16),
            pltpu.VMEM((32, RANK, PART), bf16),
            pltpu.VMEM((RANK, PART), bf16),
            pltpu.VMEM((RING, 8, count), f32),
            pltpu.VMEM((RING, 8, count), f32),
            pltpu.VMEM((7, count, width // 2), bf16),
            pltpu.VMEM((7, count, width // 2), bf16),
            pltpu.VMEM((4, RANK, units), f32),
            pltpu.VMEM((4, rows, units), f32),
            pltpu.VMEM((4, rows, units), f32),
            pltpu.VMEM((4, rows, units), bf16),
            pltpu.VMEM((4, rows, RANK), bf16),
            dma((2, 2, 4, 2)),
            dma((2, 8, 2)),
            dma((3,)),
            dma((3,)),
            dma((6, 8)),
            dma((6, 8)),
            dma((2, 4, 2)),
            dma((2, 4, 2)),
            dma,
            dma,
            dma,
            dma,
            dma,
            dma,
            dma((5,)),
        ],
        compiler_params=pltpu.CompilerParams(
            collective_id=0, has_side_effects=True, vmem_limit_bytes=60 * 1024 * 1024
        ),
        name="expert_layer",
    )(tokens, grads, chosen, weights, gate, up, down, first, second)


def decoupled_adam_update(param, grad, moment, second):
    moment_new = beta_one * moment + (1.0 - beta_one) * grad
    second_new = beta_two * second + (1.0 - beta_two) * grad * grad
    update = (
        moment_new / bias_one / (jnp.sqrt(second_new / bias_two) + adam_eps) + weight_decay * param
    )
    return (moment_new, second_new, update)


def shards(
    tokens,
    output_gradient,
    chosen_expert_index,
    router_weight,
    gate_weight,
    up_weight,
    down_weight,
    adapter_down_first,
    adapter_down_second,
    first_mean_a,
    squared_mean_a,
    first_mean_b,
    squared_mean_b,
):
    unit_count = adapter_down_first.shape[1]
    token_grad, sums = expert_layer(
        tokens,
        output_gradient,
        chosen_expert_index.T,
        router_weight.T,
        jnp.swapaxes(gate_weight, 1, 2),
        jnp.swapaxes(up_weight, 1, 2),
        down_weight,
        jnp.swapaxes(adapter_down_first, 1, 2),
        adapter_down_second,
    )
    updated_a = decoupled_adam_update(
        adapter_down_first[0], sums[:, :unit_count].T, first_mean_a[0], squared_mean_a[0]
    )
    updated_b = decoupled_adam_update(
        adapter_down_second[0], sums[:, 128:], first_mean_b[0], squared_mean_b[0]
    )
    return (token_grad, *(v[None] for v in updated_a), *(v[None] for v in updated_b))


def solution(mesh):
    rows = P(("dp", "expert"), None)
    frozen = P("expert", None, None)
    first = P("expert", "dp", None)
    second = P("expert", None, "dp")
    return jax.shard_map(
        shards,
        mesh=mesh,
        in_specs=(rows,) * 4 + (frozen,) * 3 + (first, second, first, first, second, second),
        out_specs=(rows, first, first, first, second, second, second),
        check_vma=False,
    )
```

```python
import functools
import math

import jax
import jax.numpy as jnp
from jax import lax
from jax.experimental import pallas as pl
from jax.experimental.pallas import tpu as pltpu
from jax.sharding import PartitionSpec as P

adapter_scale = 2.0
beta_one = 0.9
beta_two = 0.999
bias_one = 1.0 - math.exp(1000.0 * math.log(0.9))
bias_two = 1.0 - math.exp(1000.0 * math.log(0.999))
adam_eps = 1e-08
weight_decay = 0.1

MESH = pl.DeviceIdType.MESH
NT = (((1,), (1,)), ((), ()))
NN = (((1,), (0,)), ((), ()))
TN = (((0,), (0,)), ((), ()))
RING = 8
SLOT = 32
RANK = 32
PART = 384
f32 = jnp.float32
bf16 = jnp.bfloat16


def dot(a, b, dims=NN):
    return lax.dot_general(a, b, dims, preferred_element_type=f32)


def kernel(
    tok_ref, grad_ref, chosen_ref, weight_ref, gate_ref, up_ref, down_ref, first_ref, second_ref,
    out_ref, sum_ref,
    tg, wg, wu, wd, ab, gr, shard, ms, mr, rp, rm, factor, act, slope, hid, lg,
    ag_send, ag_recv, own_send, own_recv, w_send, w_recv, rs_send, rs_recv, ab_send, ab_recv,
    gab_send, gab_recv, m_send, m_recv, own_sem,
):
    tokens, width = tok_ref.shape
    units = gate_ref.shape[1]
    half = width // 2
    eighth = width // 8
    unit_count = units // 8
    dp = lax.axis_index("dp")
    ex = lax.axis_index("expert")
    z, xh, core = ex // 4, (ex // 2) % 2, ex % 2
    y, xl = dp // 2, dp % 2

    def at(zz, hh, cc):
        return (zz * 2 + hh) * 2 + cc

    zp = (dp, at((z + 1) % RING, xh, core))
    zm = (dp, at((z + RING - 1) % RING, xh, core))
    sib = (dp, at(z, xh, 1 - core))
    cross = (y * 2 + 1 - xl, at(z, 1 - xh, core))
    xlo = (y * 2 + 1 - xl, ex)
    yp = (((y + 1) % 4) * 2 + xl, ex)
    ym = (((y + 3) % 4) * 2 + xl, ex)

    def plane(k, j):
        hh = xh if k < 2 else 1 - xh
        cc = core if k % 2 == 0 else 1 - core
        return ((dp + j) % 8, at(z, hh, cc))

    def each_peer(f):
        for k in range(4):
            lax.fori_loop(1 if k == 0 else 0, 8, functools.partial(lambda k, j, c: (f(k, j), c)[1], k), 0)

    barrier = pltpu.get_barrier_semaphore()

    def greet(device):
        pl.semaphore_signal(barrier, inc=1, device_id=device, device_id_type=MESH)

    each_peer(lambda k, j: greet(plane(k, j)))
    lax.fori_loop(1, RING, lambda r, c: (greet((dp, at((z + r) % RING, xh, core))), c)[1], 0)
    pl.semaphore_wait(barrier, 31 + RING - 1)

    def remote(src, dst, send, recv, device):
        return pltpu.make_async_remote_copy(
            src_ref=src, dst_ref=dst, send_sem=send, recv_sem=recv, device_id=device, device_id_type=MESH
        )

    def sl(r):
        return (r + 2) % RING

    def piece(ref, h):
        return ref.at[:, pl.ds(h * half, half)]

    def ag(a, way, hop, h):
        own = tok_ref if a == 0 else grad_ref
        here = hop if way == 0 else RING - hop
        there = hop + 1 if way == 0 else RING - hop - 1
        src = own if hop == 0 else tg.at[a, sl(here)]
        return remote(
            piece(src, h), piece(tg.at[a, sl(there)], h), ag_send.at[a, way, hop, h],
            ag_recv.at[a, there, h], zp if way == 0 else zm,
        )

    def ag_has(hop, way, h):
        return hop < 3 or h == way

    def ag_own(a):
        for h in range(2):
            for way in range(2):
                ag(a, way, 0, h).start()

    def ag_arrive(a, hop, h):
        for way in range(2):
            if ag_has(hop - 1, way, h):
                ag(a, way, hop - 1, h).wait_recv()
                if hop < 4 and ag_has(hop, way, h):
                    ag(a, way, hop, h).start()

    def ag_sent(a, hops):
        for hop in hops:
            for h in range(2):
                for way in range(2):
                    if ag_has(hop, way, h):
                        ag(a, way, hop, h).wait_send()

    own_w = (gate_ref.at[0], up_ref.at[0], down_ref.at[0])
    all_w = (wg, wu, wd)
    mine = (y % 2) * 2
    other = 2 - mine

    def w_copy(i, n):
        m, j = i // 2, i % 2
        quarter = (
            mine + 1 - xl, mine + xl, mine + xl, mine + 1 - xl,
            mine + xl, mine + 1 - xl, other + xl, other + 1 - xl,
        )[n]
        cols = pl.ds(pl.multiple_of((quarter * 2 + j) * eighth, eighth), eighth)
        src = own_w[m] if n == 0 else all_w[m].at[2]
        dst = all_w[m].at[2 if n < 4 else 3]
        device = (cross, xlo, ym, yp, sib, sib, sib, sib)[n]
        return remote(src.at[:, cols], dst.at[:, cols], w_send.at[i, n], w_recv.at[i, n], device)

    def w_own(m):
        return remote(own_w[m], all_w[m].at[1], own_send.at[m], own_recv.at[m], sib)

    def w_first(i):
        w_copy(i, 0).wait_recv()
        for n in (1, 2, 4):
            w_copy(i, n).start()
        if i < 4:
            w_copy(i + 2, 0).start()

    def w_second(i):
        w_copy(i, 1).wait_recv()
        for n in (3, 5):
            w_copy(i, n).start()
        w_copy(i, 2).wait_recv()
        w_copy(i, 6).start()

    def w_third(i):
        w_copy(i, 3).wait_recv()
        w_copy(i, 7).start()

    def w_have(some):
        for i in some:
            for n in (4, 5, 6, 7):
                w_copy(i, n).wait_recv()

    ag_own(0)
    w_copy(0, 0).start()
    w_copy(1, 0).start()
    own_copies = [pltpu.make_async_copy(own_w[m], all_w[m].at[0], own_sem.at[2 + m]) for m in range(3)]
    own_tok = pltpu.make_async_copy(tok_ref, tg.at[0, sl(0)], own_sem.at[0])
    own_grad = pltpu.make_async_copy(grad_ref, tg.at[1, sl(0)], own_sem.at[1])
    own_tok.start()
    own_grad.start()
    for m in range(3):
        w_own(m).start()
        own_copies[m].start()

    shard[...] = jnp.zeros_like(shard)
    shard[:, 0:unit_count] = first_ref[0].astype(bf16)
    shard[:, 128:PART] = second_ref[0].astype(bf16)
    ab[pl.ds(dp, 1)] = shard[...][None]

    def ab_copy(k, j):
        return remote(shard, ab.at[k * 8 + dp], ab_send, ab_recv, plane(k, j))


    ids = lax.broadcasted_iota(jnp.int32, (4 * RING, tokens), 0)
    named = jnp.zeros((4 * RING, tokens), f32)
    weighted = jnp.zeros((4 * RING, tokens), f32)
    for k in range(chosen_ref.shape[0]):
        hit = ids == chosen_ref[k : k + 1, :]
        named = jnp.where(hit, 1.0, named)
        weighted = jnp.where(hit, weight_ref[k : k + 1, :], weighted)
    earlier = lax.broadcasted_iota(jnp.int32, (tokens, tokens), 0) < lax.broadcasted_iota(
        jnp.int32, (tokens, tokens), 1
    )
    rank = dot(named.astype(bf16), jnp.where(earlier, 1.0, 0.0).astype(bf16))
    rank = jnp.where(named > 0.5, rank, -1.0)
    for zz in range(RING):
        ms[zz, 0:4, :] = rank[zz * 4 : zz * 4 + 4]
        ms[zz, 4:8, :] = weighted[zz * 4 : zz * 4 + 4]
    mr[pl.ds(sl(0), 1)] = ms[pl.ds(z, 1)]

    def m_copy(r):
        there = (z + r) % RING
        return remote(ms.at[there], mr.at[sl(r)], m_send, m_recv, (dp, at(there, xh, core)))

    lax.fori_loop(1, RING, lambda r, c: (m_copy(r).start(), c)[1], 0)

    def spread(d):
        i = lax.broadcasted_iota(jnp.int32, (128, units), 0)
        j = lax.broadcasted_iota(jnp.int32, (128, units), 1)
        return jnp.where((j - d * unit_count == i) & (i < unit_count), 1.0, 0.0).astype(bf16)

    def assemble(d, carry):
        one = spread(d)
        for k in range(4):
            factor[k] = factor[k] + dot(ab[k * 8 + d, :, 0:128], one)
        return carry

    slots = lax.broadcasted_iota(jnp.int32, (SLOT, tokens), 0).astype(f32)

    def row_of(k):
        hh = xh if k < 2 else 1 - xh
        cc = core if k % 2 == 0 else 1 - core
        return hh * 2 + cc

    def picks(b):
        return [jnp.where(slots == mr[b, pl.ds(row_of(k), 1), :], 1.0, 0.0) for k in range(4)]

    def gather_tokens(b, carry):
        tg[0, b] = dot(jnp.concatenate(picks(b), axis=0).astype(bf16), tg[0, b]).astype(bf16)
        return carry

    def gather_grads(b, carry):
        chosen = picks(b)
        scale = jnp.concatenate(
            [
                jnp.sum(chosen[k] * mr[b, pl.ds(row_of(k) + 4, 1), :], axis=1, keepdims=True)
                for k in range(4)
            ],
            axis=0,
        )
        pick = jnp.concatenate(chosen, axis=0).astype(bf16)
        tg[1, b] = (dot(pick, tg[1, b]) * scale).astype(bf16)
        return carry

    def over(begin, end, f):
        for k in range(begin, end):
            f(k, 0)

    def pairwise(f):
        def two(i, carry):
            f(2 * i, 0)
            return f(2 * i + 1, carry)

        return two

    def rows_of(k):
        if isinstance(k, int):
            return slice(k * SLOT, (k + 1) * SLOT)
        return pl.ds(pl.multiple_of(k * SLOT, SLOT), SLOT)

    def forward(k, carry):
        x = tg[0, :, rows_of(k), :].reshape(RING * SLOT, width)
        gate_pre = dot(x, wg[k], NT)
        up_pre = dot(x, wu[k], NT)
        s = jax.nn.sigmoid(gate_pre)
        activated = gate_pre * s
        act[k] = activated
        hid[k] = (activated * up_pre).astype(bf16)
        slope[k] = up_pre * s * (1.0 + gate_pre * (1.0 - s))
        return carry

    def second_factor(k):
        return jnp.concatenate([ab[k * 8 + d, :, 128:PART] for d in range(8)], axis=1)

    def backward(first, blocks):
        rows = slice(first * SLOT, (first + blocks) * SLOT)
        near = slice(first, first + blocks)

        def one(k, carry):
            g = tg[1, near, rows_of(k), :].reshape(blocks * SLOT, width)
            low_grad = dot(g, second_factor(k), NT).astype(bf16)
            lg[k, rows, :] = low_grad
            hidden_grad = dot(g, wd[k], NT) + adapter_scale * dot(low_grad, factor[k].astype(bf16))
            gate_grad = (hidden_grad * slope[k, rows, :]).astype(bf16)
            up_grad = (hidden_grad * act[k, rows, :]).astype(bf16)
            pair = dot(gate_grad, wg[k]) + dot(up_grad, wu[k])
            tg[0, near, rows_of(k), :] = pair.astype(bf16).reshape(blocks, SLOT, width)
            return carry

        return one

    far = slice(5 * SLOT, RING * SLOT)

    def far_slopes(k, carry):
        g = tg[1, 5:RING, rows_of(k), :].reshape(3 * SLOT, width)
        low_grad = dot(g, second_factor(k), NT).astype(bf16)
        lg[k, far, :] = low_grad
        hidden_grad = dot(g, wd[k], NT) + adapter_scale * dot(low_grad, factor[k].astype(bf16))
        slope[k, far, :] = (hidden_grad * slope[k, far, :]).astype(bf16).astype(f32)
        act[k, far, :] = (hidden_grad * act[k, far, :]).astype(bf16).astype(f32)
        return carry

    def far_pairs(h):
        cols = slice(h * half, h * half + half)

        def one(k, carry):
            pair = dot(slope[k, far, :].astype(bf16), wg[k, :, cols]) + dot(
                act[k, far, :].astype(bf16), wu[k, :, cols]
            )
            tg[0, 5:RING, rows_of(k), cols] = pair.astype(bf16).reshape(3, SLOT, half)
            return carry

        def sums(b, carry):
            pick = jnp.concatenate(picks(b), axis=0).astype(bf16)
            tg[0, b, :, cols] = dot(pick, tg[0, b, :, cols], TN).astype(bf16)
            return carry

        over(0, 4, one)
        over(5, RING, sums)

    def combine(b, carry):
        pick = jnp.concatenate(picks(b), axis=0).astype(bf16)
        tg[0, b] = dot(pick, tg[0, b], TN).astype(bf16)
        return carry

    def adapter_grads(k, carry):
        g = tg[1, :, rows_of(k), :].reshape(RING * SLOT, width)
        low_rank = dot(hid[k], factor[k].astype(bf16), NT).astype(bf16)
        grad_a = (adapter_scale * dot(lg[k], hid[k], TN)).astype(bf16)
        grad_b = (adapter_scale * dot(low_rank, g, TN)).astype(bf16)
        for d in range(8):
            ab[k * 8 + d, :, 0:128] = dot(grad_a, spread(d), NT).astype(bf16)
            ab[k * 8 + d, :, 128:PART] = grad_b[:, d * 256 : d * 256 + 256]
        return carry

    ag_arrive(0, 1, 0)
    w_first(0)
    ag_arrive(0, 1, 1)
    w_first(1)
    ag_arrive(0, 2, 0)
    w_second(0)
    ag_arrive(0, 2, 1)
    w_first(2)
    each_peer(lambda k, j: ab_copy(k, j).start())
    w_second(1)
    ag_arrive(0, 3, 0)
    w_third(0)
    ag_arrive(0, 3, 1)
    ag_own(1)
    w_first(3)
    w_second(2)
    own_tok.wait()
    own_grad.wait()
    seven = mr.at[pl.ds(0, RING - 1)]
    pltpu.make_async_copy(seven, seven, m_recv).wait()
    pltpu.make_async_copy(seven, seven, m_send).wait()
    ag_arrive(0, 4, 0)
    ag_arrive(0, 4, 1)

    w_third(1)
    w_first(4)
    w_second(3)
    ag_sent(0, range(4))
    ag_arrive(1, 1, 0)
    w_third(2)
    lax.fori_loop(0, RING // 2, pairwise(gather_tokens), 0)
    w_first(5)
    ag_arrive(1, 1, 1)
    for m in range(3):
        own_copies[m].wait()
        w_own(m).wait_recv()
    over(0, 2, forward)
    w_second(4)
    w_third(3)
    ag_arrive(1, 2, 0)
    w_have((0, 1, 2, 3))
    over(2, 4, forward)
    w_second(5)
    w_third(4)
    ag_arrive(1, 2, 1)
    many = ab.at[pl.ds(0, 31)]
    pltpu.make_async_copy(many, many, ab_recv).wait()
    pltpu.make_async_copy(many, many, ab_send).wait()
    factor[...] = jnp.zeros_like(factor)
    lax.fori_loop(0, 8, assemble, 0)
    ag_sent(1, (1, 2))
    lax.fori_loop(0, 2, pairwise(gather_grads), 0)
    gather_grads(4, 0)
    w_third(5)
    ag_arrive(1, 3, 0)
    over(0, 2, backward(0, 5))
    ag_arrive(1, 3, 1)
    w_have((4, 5))
    over(2, 4, backward(0, 5))
    ag_arrive(1, 4, 0)
    ag_arrive(1, 4, 1)
    ag_sent(1, (0, 3))
    over(5, RING, gather_grads)
    over(0, 4, far_slopes)

    def landing(way, step, h):
        return (rp if way == 0 else rm).at[0 if step == 0 else 2 * step - 1 + h]

    def rs(way, step, h):
        here = 4 + step if way == 0 else 4 - step
        return remote(
            piece(tg.at[0, sl(here)], h), landing(way, step, h), rs_send.at[way, step, h],
            rs_recv.at[way, step, h], zp if way == 0 else zm,
        )

    def rs_add(way, step, h):
        rs(way, step, h).wait_recv()
        here = sl(5 + step if way == 0 else 3 - step)
        cols = slice(h * half, h * half + half)
        tg[0, here, :, cols] = (
            tg[0, here, :, cols].astype(f32) + landing(way, step, h)[...].astype(f32)
        ).astype(bf16)
        rs(way, step + 1, h).start()

    for h in range(2):
        far_pairs(h)
        rs(h, 0, h).start()
        rs(1 - h, 1, h).start()
    lax.fori_loop(0, 2, pairwise(combine), 0)
    combine(4, 0)
    for way in range(2):
        rs_add(way, 0, way)
    lax.fori_loop(0, 2, adapter_grads, 0)
    for way in range(2):
        rs_add(way, 1, 1 - way)
    lax.fori_loop(2, 4, adapter_grads, 0)

    def gab_copy(k, j):
        return remote(ab.at[k * 8 + (dp + j) % 8], gr.at[k * 8 + dp], gab_send, gab_recv, plane(k, j))

    each_peer(lambda k, j: gab_copy(k, j).start())
    for way in range(2):
        rs_add(way, 1, way)
    for way in range(2):
        rs_add(way, 2, 1 - way)
    for way in range(2):
        rs_add(way, 2, way)

    many_g = gr.at[pl.ds(0, 31)]
    pltpu.make_async_copy(many_g, many_g, gab_recv).wait()
    pltpu.make_async_copy(many_g, many_g, gab_send).wait()
    gr[pl.ds(dp, 1)] = ab[pl.ds(dp, 1)]
    sum_ref[...] = lax.fori_loop(
        0, 32, lambda i, total: total + gr[i].astype(f32), jnp.zeros((RANK, PART), f32)
    )
    for i in range(6):
        for n in range(8):
            w_copy(i, n).wait_send()
    for m in range(3):
        w_own(m).wait_send()
    for h in (1, 0):
        rs(0, 3, h).wait_recv()
        rs(1, 3, h).wait_recv()
        cols = slice(h * half, h * half + half)
        out_ref[:, cols] = (
            tg[0, sl(0), :, cols].astype(f32)
            + landing(0, 3, h)[...].astype(f32)
            + landing(1, 3, h)[...].astype(f32)
        ).astype(bf16)
    for way in range(2):
        for step in range(4):
            for h in range(2):
                if step > 0 or h == way:
                    rs(way, step, h).wait_send()


def expert_layer(tokens, grads, chosen, weights, gate, up, down, first, second):
    count, width = tokens.shape
    units = gate.shape[1]
    rows = RING * SLOT
    vmem = pl.BlockSpec(memory_space=pltpu.VMEM)
    hbm = pl.BlockSpec(memory_space=pl.ANY)
    dma = pltpu.SemaphoreType.DMA
    return pl.pallas_call(
        kernel,
        out_shape=(
            jax.ShapeDtypeStruct((count, width), bf16),
            jax.ShapeDtypeStruct((RANK, PART), f32),
        ),
        in_specs=[hbm, hbm, vmem, vmem, hbm, hbm, hbm, vmem, vmem],
        out_specs=(vmem, vmem),
        scratch_shapes=[
            pltpu.VMEM((2, RING, count, width), bf16),
            pltpu.VMEM((4, units, width), bf16),
            pltpu.VMEM((4, units, width), bf16),
            pltpu.VMEM((4, units, width), bf16),
            pltpu.VMEM((32, RANK, PART), bf16),
            pltpu.VMEM((32, RANK, PART), bf16),
            pltpu.VMEM((RANK, PART), bf16),
            pltpu.VMEM((RING, 8, count), f32),
            pltpu.VMEM((RING, 8, count), f32),
            pltpu.VMEM((7, count, width // 2), bf16),
            pltpu.VMEM((7, count, width // 2), bf16),
            pltpu.VMEM((4, RANK, units), f32),
            pltpu.VMEM((4, rows, units), f32),
            pltpu.VMEM((4, rows, units), f32),
            pltpu.VMEM((4, rows, units), bf16),
            pltpu.VMEM((4, rows, RANK), bf16),
            dma((2, 2, 4, 2)),
            dma((2, 8, 2)),
            dma((3,)),
            dma((3,)),
            dma((6, 8)),
            dma((6, 8)),
            dma((2, 4, 2)),
            dma((2, 4, 2)),
            dma,
            dma,
            dma,
            dma,
            dma,
            dma,
            dma((5,)),
        ],
        compiler_params=pltpu.CompilerParams(
            collective_id=0, has_side_effects=True, vmem_limit_bytes=60 * 1024 * 1024
        ),
        name="expert_layer",
    )(tokens, grads, chosen, weights, gate, up, down, first, second)


def decoupled_adam_update(param, grad, moment, second):
    moment_new = beta_one * moment + (1.0 - beta_one) * grad
    second_new = beta_two * second + (1.0 - beta_two) * grad * grad
    update = (
        moment_new / bias_one / (jnp.sqrt(second_new / bias_two) + adam_eps) + weight_decay * param
    )
    return (moment_new, second_new, update)


def shards(
    tokens,
    output_gradient,
    chosen_expert_index,
    router_weight,
    gate_weight,
    up_weight,
    down_weight,
    adapter_down_first,
    adapter_down_second,
    first_mean_a,
    squared_mean_a,
    first_mean_b,
    squared_mean_b,
):
    unit_count = adapter_down_first.shape[1]
    token_grad, sums = expert_layer(
        tokens,
        output_gradient,
        chosen_expert_index.T,
        router_weight.T,
        jnp.swapaxes(gate_weight, 1, 2),
        jnp.swapaxes(up_weight, 1, 2),
        down_weight,
        jnp.swapaxes(adapter_down_first, 1, 2),
        adapter_down_second,
    )
    updated_a = decoupled_adam_update(
        adapter_down_first[0], sums[:, :unit_count].T, first_mean_a[0], squared_mean_a[0]
    )
    updated_b = decoupled_adam_update(
        adapter_down_second[0], sums[:, 128:], first_mean_b[0], squared_mean_b[0]
    )
    return (token_grad, *(v[None] for v in updated_a), *(v[None] for v in updated_b))


def solution(mesh):
    rows = P(("dp", "expert"), None)
    frozen = P("expert", None, None)
    first = P("expert", "dp", None)
    second = P("expert", None, "dp")
    return jax.shard_map(
        shards,
        mesh=mesh,
        in_specs=(rows,) * 4 + (frozen,) * 3 + (first, second, first, first, second, second),
        out_specs=(rows, first, first, first, second, second, second),
        check_vma=False,
    )
```
